256 devices in a mesh: rep: 32 (over y, x, core), head: 8 (over z).
Axes of the slice: x: 4, y: 4, z: 8, core: 2. Of those that a mesh axis runs over, the one named last changes fastest.
Arguments:
- states: float32 [256, 32, 128, 128], P('rep', 'head'), may hold values from -6 to 6
- alive_flag: int32 [256], P('rep'), may hold values from 0 to 1, as said below
- plan_source: int32 [32, 3], replicated, may hold values from 0 to 7, as said below
- plan_target: int32 [32, 3], replicated, may hold values from 0 to 255, as said below
- move_count: int32 [32], replicated, may hold values from 2 to 3, as said below
- query_proj: bfloat16 [256, 4, 4096], P('rep', None, 'head'), may hold values from -6 to 6
- key_proj: bfloat16 [256, 4, 4096], P('rep', None, 'head'), may hold values from -6 to 6
- value_proj: bfloat16 [256, 4, 4096], P('rep', None, 'head'), may hold values from -6 to 6
- gate_proj: bfloat16 [256, 4, 4096], P('rep', None, 'head'), may hold values from -8 to 8
- decay_rate: float32 [32], P('head'), may hold values from 0.02 to 2
- norm_gain: float32 [4096], P('head'), may hold values from 0.1 to 1.9
Outputs:
- attended: bfloat16 [256, 4, 4096], P('rep', None, 'head')
- new_states: float32 [256, 32, 128, 128], P('rep', 'head')
The draws below stay inside these ranges and needn't reach their ends.
Inputs may be any that keep to these rules, and one draw needn't show every extreme that they name: `alive_flag`: 1 marks a slot whose row is unfinished before the moves. `plan_source`: for a move in force, the anchor slot is alive and differs from the replica's other anchors in force; other entries are in range and meaningless. `plan_target`: for a move (r, m) in force with g = m // 2, the target is a slot whose alive_flag is 0 on replica (r + d) mod 32, where d = 16 for g = 0 and d = g otherwise; no slot is the target of two moves in force. Other entries are in range and meaningless. `move_count`: the value 3 is reached on some replica in every draw.
All inputs are finite; a program needn't handle non-finite values.
Results may differ from the reference program's by a relative error of at most 0.0011.
Values sent between devices are 32-bit elements; how exact they have to be, the bound alone decides.
No kernel may reach another device: no remote copies, remote signals or barrier semaphores. Data moves between devices by JAX's collectives and lax.ppermute only.
A program may use at most 128 MiB of HBM per device.

```python
import math
import jax
import jax.numpy as jnp
from jax import lax

SLOTS_DEV = 8
MOVE = 3
CAP = 2
STEPS = 4
HEADS = 32
DK = 128
HD = 4096
SLOTS = 256
N_REP = 32


def make_plan(key):
    key_list = jax.random.split(key, 4)
    slot_keys = jax.random.split(key_list[0], N_REP)
    slot_perm = jax.vmap(lambda one_key: jax.random.permutation(one_key, SLOTS_DEV))(slot_keys).astype(jnp.int32)
    rep_ids = jnp.arange(N_REP, dtype=jnp.int32)
    counts = jax.random.randint(key_list[1], (N_REP,), 2, MOVE + 1).astype(jnp.int32)
    full_rep = jax.random.randint(key_list[2], (), 0, N_REP).astype(jnp.int32)
    counts = jnp.where(rep_ids == full_rep, MOVE, counts).astype(jnp.int32)
    move_ids = jnp.arange(MOVE, dtype=jnp.int32)
    group = move_ids // CAP
    distance = jnp.where(group == 0, N_REP // 2, group).astype(jnp.int32)
    taker_rep = (rep_ids[:, None] + distance[None, :]) % N_REP
    free_place = jnp.broadcast_to(MOVE + move_ids[None, :], taker_rep.shape)
    plan_target = (taker_rep * SLOTS_DEV + slot_perm[taker_rep, free_place]).astype(jnp.int32)
    plan_source = slot_perm[:, :MOVE]
    slot_place = jnp.argsort(slot_perm, axis=1).astype(jnp.int32)
    extra_live = jax.random.randint(key_list[3], (N_REP, SLOTS_DEV), 0, 4) > 0
    alive_rows = (slot_place < MOVE) | (slot_place >= 2 * MOVE) & extra_live
    return (alive_rows.reshape(-1).astype(jnp.int32), plan_source, plan_target, counts)


def draw_alive_flag(key, part):
    return make_plan(key)[0]


def draw_plan_source(key, part):
    return make_plan(key)[1]


def draw_plan_target(key, part):
    return make_plan(key)[2]


def draw_move_count(key, part):
    return make_plan(key)[3]


def shard_levels(rng, shape, cuts, smallest, top_value):
    def one(axis_at, blocks):
        steps = jax.random.uniform(jax.random.fold_in(jax.random.fold_in(rng, 6), axis_at), (blocks,), jnp.float32, smallest / len(cuts), top_value / len(cuts))
        return jnp.repeat(jnp.exp(steps), shape[axis_at] // blocks).reshape((-1,) + (1,) * (len(shape) - axis_at - 1))

    factor_of = one(*cuts[0])
    for cut in cuts[1:]:
        factor_of = factor_of * one(*cut)
    return factor_of


def normal_values(stream_key, shape, spread, limit, cuts=(), kind=jnp.bfloat16):
    level = shard_levels(stream_key, shape, cuts, -0.22, 0.18) if cuts else 1.0
    entries = jax.random.normal(stream_key, shape, jnp.float32) * spread * level
    return jnp.minimum(jnp.maximum(entries, -limit), limit).astype(kind)


def setup_inputs(seed: int = 0) -> dict:
    keys = jax.random.split(jax.random.key(seed), 12)
    return {
        "states": normal_values(keys[0], (SLOTS, HEADS, DK, DK), 1.0, 6.0, ((0, 32), (1, 8)), jnp.float32),
        "alive_flag": draw_alive_flag(jax.random.fold_in(keys[11], 71), 0),
        "plan_source": draw_plan_source(jax.random.fold_in(keys[11], 71), 0),
        "plan_target": draw_plan_target(jax.random.fold_in(keys[11], 71), 0),
        "move_count": draw_move_count(jax.random.fold_in(keys[11], 71), 0),
        "query_proj": normal_values(keys[5], (SLOTS, STEPS, HD), 1.0, 6.0, ((0, 32), (2, 8))),
        "key_proj": normal_values(keys[6], (SLOTS, STEPS, HD), 1.0, 6.0, ((0, 32), (2, 8))),
        "value_proj": normal_values(keys[7], (SLOTS, STEPS, HD), 1.0, 6.0, ((0, 32), (2, 8))),
        "gate_proj": normal_values(keys[8], (SLOTS, STEPS, HD), 1.5, 8.0, ((0, 32), (2, 8))),
        "decay_rate": jnp.clip(jnp.exp(math.log(2.0) - 4.6051702 * jax.random.uniform(keys[9], (HEADS,), jnp.float32) ** shard_levels(keys[9], (HEADS,), ((0, 8),), -0.2, 0.2)), 0.02, 2.0),
        "norm_gain": jnp.clip(1.0 + 0.18 * jax.random.normal(keys[10], (HD,), jnp.float32), 0.1, 1.9),
    }


epsilon = 1e-06

def reference(states, alive_flag, plan_source, plan_target, move_count, query_proj, key_proj, value_proj, gate_proj, decay_rate, norm_gain):
    slot_total = alive_flag.shape[0]
    per_device = slot_total // N_REP
    move_ids = jnp.arange(MOVE, dtype=jnp.int32)
    is_valid = move_ids[None, :] < move_count[:, None]
    anchor = jnp.arange(N_REP, dtype=jnp.int32)[:, None] * per_device + plan_source
    target = jnp.where(is_valid, plan_target, slot_total).reshape(-1)
    anchor_of = jnp.zeros((slot_total,), jnp.int32).at[target].set(anchor.reshape(-1), mode='drop')
    arrives = jnp.zeros((slot_total,), jnp.int32).at[target].set(1, mode='drop')
    leaving_at = jnp.where(is_valid, anchor, slot_total).reshape(-1)
    leaves = jnp.zeros((slot_total,), jnp.int32).at[leaving_at].set(1, mode='drop')
    staying = alive_flag * (1 - leaves)
    live_rows = arrives + staying

    def activate(projection):
        return jax.nn.silu(projection.astype(jnp.float32)).reshape(slot_total, STEPS, HEADS, DK)
    queries = activate(query_proj)
    keys_now = activate(key_proj)
    values_now = activate(value_proj)

    def per_head(head_index, loop_carry):
        finals, readouts = loop_carry
        initial = lax.dynamic_index_in_dim(states, head_index, 1, keepdims=False)
        moved_rows = jnp.take(initial, anchor_of, axis=0)
        current = jnp.where(arrives[:, None, None] == 1, moved_rows, jnp.where(staying[:, None, None] == 1, initial, jnp.zeros_like(initial)))
        factor = jnp.exp(-lax.dynamic_index_in_dim(decay_rate, head_index, 0, keepdims=False))
        head_query = lax.dynamic_index_in_dim(queries, head_index, 2, keepdims=False)
        head_key = lax.dynamic_index_in_dim(keys_now, head_index, 2, keepdims=False)
        head_value = lax.dynamic_index_in_dim(values_now, head_index, 2, keepdims=False)
        outputs = []
        for step_index in range(STEPS):
            current = factor * current + head_key[:, step_index, :, None] * head_value[:, step_index, None, :]
            outputs.append(jnp.einsum('sd,sde->se', head_query[:, step_index], current, precision=lax.Precision.HIGHEST))
        finals = lax.dynamic_update_index_in_dim(finals, current, head_index, 1)
        readouts = lax.dynamic_update_index_in_dim(readouts, jnp.stack(outputs, 1), head_index, 2)
        return (finals, readouts)
    finals, readouts = lax.fori_loop(0, HEADS, per_head, (jnp.zeros(states.shape, jnp.float32), jnp.zeros((slot_total, STEPS, HEADS, DK), jnp.float32)))
    readout_rows = readouts.reshape(slot_total, STEPS, HEADS * DK)
    inverse_rms = lax.rsqrt(lax.optimization_barrier(jnp.mean(readout_rows * readout_rows, axis=2, keepdims=True)) + epsilon)
    gated_rows = readout_rows * inverse_rms * norm_gain * jax.nn.sigmoid(gate_proj.astype(jnp.float32))
    live_float = live_rows.astype(jnp.float32)
    attended = (gated_rows * live_float[:, None, None]).astype(jnp.bfloat16)
    new_states = finals * live_float[:, None, None, None]
    return (attended, new_states)
```

```python
import jax
import jax.numpy as jnp
from jax import lax
from jax.experimental import pallas as pl
from jax.experimental.pallas import tpu as pltpu
from jax.sharding import PartitionSpec as P

SLOTS_DEV = 8
MOVE = 3
STEPS = 4
N_REP = 32
N_HEAD = 8
HEADS = 32
DK = 128
HEADS_DEV = HEADS // N_HEAD
WIDTH = HEADS_DEV * DK
FAR = N_REP // 2
epsilon = 1e-06

HIGHEST = lax.Precision.HIGHEST
VMEM = pl.BlockSpec(memory_space=pltpu.VMEM)
SMEM = pl.BlockSpec(memory_space=pltpu.SMEM)
ANY = pl.BlockSpec(memory_space=pl.ANY)


def silu(x):
    x = x.astype(jnp.float32)
    return x / (1.0 + jnp.exp(-x))


def sender_of(move):
    me = lax.axis_index("rep")
    return lax.rem(me + (FAR if move < 2 else N_REP - 1), N_REP)


def comes_to(move, target_ref, count_ref):
    sender = sender_of(move)
    return count_ref[sender] > move, lax.rem(target_ref[sender, move], SLOTS_DEV)


def slot_flags(slot, alive_ref, source_ref, target_ref, count_ref):
    me = lax.axis_index("rep")
    leaves = False
    arrives = False
    for move in range(MOVE):
        leaves |= (count_ref[me] > move) & (source_ref[me, move] == slot)
        valid, at = comes_to(move, target_ref, count_ref)
        arrives |= valid & (at == slot)
    return (alive_ref[slot] == 1) & jnp.logical_not(leaves), arrives


def step_column(height=STEPS):
    return lax.broadcasted_iota(jnp.int32, (height, DK), 0).astype(jnp.float32)


def head_slice(head):
    return slice(head * DK, (head + 1) * DK)


def ask_kernel(target_ref, count_ref, query_ref, out_ref):
    for move in range(2):
        _, slot = comes_to(move, target_ref, count_ref)
        out_ref[move] = silu(query_ref[slot])


def outbox_kernel(source_ref, states_ref, far_ref, near_ref, sems):
    me = lax.axis_index("rep")
    copies = []
    for move in range(MOVE):
        out = far_ref.at[move] if move < 2 else near_ref.at[0]
        copies.append(pltpu.make_async_copy(states_ref.at[source_ref[me, move]], out, sems.at[move]))
    for copy in copies:
        copy.start()
    for copy in copies:
        copy.wait()


def answer_kernel(query_ref, far_ref, out_ref):
    for move in range(2):
        for head in range(HEADS_DEV):
            out_ref[move, :, head_slice(head)] = jnp.dot(
                query_ref[move, :, head_slice(head)], far_ref[move, head],
                precision=HIGHEST, preferred_element_type=jnp.float32)


def main_kernel(alive_ref, source_ref, target_ref, count_ref, rate_ref, query_ref, key_ref, value_ref, states_ref, out_ref, new_ref):
    slot = pl.program_id(0)
    stays, arrives = slot_flags(slot, alive_ref, source_ref, target_ref, count_ref)
    live = (stays | arrives).astype(jnp.float32)
    stays = stays.astype(jnp.float32)
    queries, keys, values = silu(query_ref[slot]), silu(key_ref[slot]), silu(value_ref[slot])
    steps = step_column()
    later = lax.broadcasted_iota(jnp.int32, (STEPS, STEPS), 0) - lax.broadcasted_iota(jnp.int32, (STEPS, STEPS), 1)
    for head in range(HEADS_DEV):
        rate = rate_ref[head]
        query, key, value = (x[:, head_slice(head)] for x in (queries, keys, values))
        state = states_ref[0, head] * stays
        weights = lax.dot_general(query, key, (((1,), (1,)), ((), ())), precision=HIGHEST, preferred_element_type=jnp.float32)
        weights = jnp.where(later >= 0, weights * jnp.exp(-rate * jnp.maximum(later, 0).astype(jnp.float32)), 0.0)
        inside = jnp.dot(weights, value, precision=HIGHEST, preferred_element_type=jnp.float32)
        before = jnp.dot(query, state, precision=HIGHEST, preferred_element_type=jnp.float32)
        out_ref[slot, :, head_slice(head)] = inside + before * jnp.exp(-rate * (steps + 1.0))
        faded = key * jnp.exp(-rate * (STEPS - 1.0 - steps))
        added = lax.dot_general(faded, value, (((0,), (0,)), ((), ())), precision=HIGHEST, preferred_element_type=jnp.float32)
        fade = jnp.exp(jnp.full((8, DK), -STEPS * rate, jnp.float32))[:1]
        new_ref[0, head] = (state * fade + added) * live


def combine_kernel(target_ref, count_ref, rate_ref, query_ref, answer_ref, near_ref, part_ref, out_ref, square_ref):
    out_ref[...] = part_ref[...]
    steps = step_column()
    for move in range(MOVE):
        valid, slot = comes_to(move, target_ref, count_ref)

        @pl.when(valid)
        def _(move=move, slot=slot):
            for head in range(HEADS_DEV):
                at = head_slice(head)
                if move < 2:
                    before = answer_ref[move, :, at]
                else:
                    before = jnp.dot(silu(query_ref[slot, :, at]), near_ref[0, head], precision=HIGHEST, preferred_element_type=jnp.float32)
                out_ref[slot, :, at] += before * jnp.exp(-rate_ref[head] * (steps + 1.0))

    total = jnp.zeros((SLOTS_DEV, STEPS, DK), jnp.float32)
    for head in range(HEADS_DEV):
        row = out_ref[:, :, head_slice(head)]
        total += row * row
    square_ref[...] = total


def final_kernel(alive_ref, source_ref, target_ref, count_ref, gain_ref, gate_ref, out_ref, square_a_ref, square_b_ref, attended_ref):
    gain = gain_ref[...]
    for slot in range(SLOTS_DEV):
        stays, arrives = slot_flags(slot, alive_ref, source_ref, target_ref, count_ref)
        live = (stays | arrives).astype(jnp.float32)
        total = jnp.sum(square_a_ref[slot] + square_b_ref[slot], axis=1, keepdims=True)
        scale = lax.rsqrt(total * (1.0 / (HEADS * DK)) + epsilon) * live
        gate = gate_ref[slot].astype(jnp.float32)
        row = out_ref[slot] * scale * gain / (1.0 + jnp.exp(-gate))
        attended_ref[slot] = row.astype(jnp.bfloat16)


def place_of(target_ref, count_ref, move):
    slots = [comes_to(m, target_ref, count_ref) for m in range(MOVE)]
    at = slots[0][1]
    for m in range(1, MOVE):
        at = jnp.where((move >= m) & slots[m][0], slots[m][1], at)
    return at


def update_kernel(target_ref, count_ref, rate_ref, far_ref, near_ref, old_ref, new_ref):
    move = pl.program_id(0)
    for m in range(MOVE):
        valid, _ = comes_to(m, target_ref, count_ref)

        @pl.when((move == m) & valid)
        def _(m=m):
            for head in range(HEADS_DEV):
                fade = jnp.exp(jnp.full((8, DK), -STEPS * rate_ref[head], jnp.float32))[:1]
                came = far_ref[0, head] if m < 2 else near_ref[0, head]
                new_ref[0, head] = old_ref[0, head] + came * fade


def call(kernel, outs, in_specs, args, cost=100_000, **more):
    if in_specs is not None:
        more["in_specs"] = in_specs
    return pl.pallas_call(
        kernel, out_shape=outs,
        cost_estimate=pl.CostEstimate(flops=cost, bytes_accessed=cost, transcendentals=0), **more,
    )(*args)


def f32(*shape):
    return jax.ShapeDtypeStruct(shape, jnp.float32)


def over_rep(x, distance):
    return lax.ppermute(x, "rep", [(i, (i + distance) % N_REP) for i in range(N_REP)])


def over_head(x, flip):
    return lax.ppermute(x, "head", [(i, i ^ flip) for i in range(N_HEAD)])


def local(states, alive_flag, plan_source, plan_target, move_count, query_proj, key_proj, value_proj, gate_proj, decay_rate, norm_gain):
    row = (HEADS_DEV, DK, DK)
    plan = (plan_target, move_count)
    flags = (alive_flag, plan_source, plan_target, move_count)
    asked = call(ask_kernel, f32(2, STEPS, WIDTH), [SMEM, SMEM, VMEM], (*plan, query_proj), out_specs=VMEM)
    asked = over_rep(asked, FAR)
    far, near = call(
        outbox_kernel, (f32(2, *row), f32(1, *row)), [SMEM, ANY], (plan_source, states), out_specs=(ANY, ANY),
        scratch_shapes=[pltpu.SemaphoreType.DMA((MOVE,))])
    near_in = over_rep(near, 1)
    far_in = over_rep(far, FAR)
    answer = call(answer_kernel, f32(2, STEPS, WIDTH), [VMEM, VMEM], (asked, far), out_specs=VMEM)
    answer = over_rep(answer, FAR)

    whole = pl.BlockSpec((SLOTS_DEV, STEPS, WIDTH), lambda i: (0, 0, 0))
    by_slot = pl.BlockSpec((1, *row), lambda i: (i, 0, 0, 0))
    part, new_states = call(
        main_kernel, (f32(SLOTS_DEV, STEPS, WIDTH), f32(SLOTS_DEV, *row)), [SMEM] * 5 + [whole] * 3 + [by_slot],
        (*flags, decay_rate, query_proj, key_proj, value_proj, states), out_specs=(whole, by_slot), grid=(SLOTS_DEV,), cost=4_000_000)
    out, square = call(
        combine_kernel, (f32(SLOTS_DEV, STEPS, WIDTH), f32(SLOTS_DEV, STEPS, DK)), [SMEM] * 3 + [VMEM] * 4,
        (*plan, decay_rate, query_proj, answer, near_in, part), out_specs=(VMEM, VMEM))
    square = square + over_head(square, 1)
    square = square + over_head(square, 2)
    other = over_head(square, 6)
    attended = call(
        final_kernel, jax.ShapeDtypeStruct((SLOTS_DEV, STEPS, WIDTH), jnp.bfloat16), [SMEM] * 4 + [VMEM] * 5,
        (*flags, norm_gain.reshape(1, WIDTH), gate_proj, out, square, other), out_specs=VMEM)
    placed = pl.BlockSpec((1, *row), lambda i, target, count: (place_of(target, count, i), 0, 0, 0))
    new_states = call(
        update_kernel, f32(SLOTS_DEV, *row), None, (*plan, decay_rate, far_in, near_in, new_states),
        cost=1_000_000, input_output_aliases={5: 0},
        grid_spec=pltpu.PrefetchScalarGridSpec(
            num_scalar_prefetch=2, grid=(MOVE,),
            in_specs=[
                SMEM,
                pl.BlockSpec((1, *row), lambda i, target, count: (jnp.minimum(i, 1), 0, 0, 0)),
                pl.BlockSpec((1, *row), lambda i, target, count: (0, 0, 0, 0)),
                placed,
            ],
            out_specs=placed))
    return attended, new_states


def solution(mesh):
    return jax.shard_map(
        local,
        mesh=mesh,
        in_specs=(
            P("rep", "head", None, None),
            P("rep"),
            P(),
            P(),
            P(),
            P("rep", None, "head"),
            P("rep", None, "head"),
            P("rep", None, "head"),
            P("rep", None, "head"),
            P("head"),
            P("head"),
        ),
        out_specs=(P("rep", None, "head"), P("rep", "head", None, None)),
        check_vma=False,
    )
```

```python
import jax
import jax.numpy as jnp
from jax import lax
from jax.experimental import pallas as pl
from jax.experimental.pallas import tpu as pltpu
from jax.sharding import PartitionSpec as P

SLOTS_DEV = 8
MOVE = 3
STEPS = 4
N_REP = 32
N_HEAD = 8
HEADS = 32
DK = 128
HEADS_DEV = HEADS // N_HEAD
WIDTH = HEADS_DEV * DK
FAR = N_REP // 2
BLOCK = 2
epsilon = 1e-06

HIGHEST = lax.Precision.HIGHEST
VMEM = pl.BlockSpec(memory_space=pltpu.VMEM)
SMEM = pl.BlockSpec(memory_space=pltpu.SMEM)
ANY = pl.BlockSpec(memory_space=pl.ANY)


def silu(x):
    x = x.astype(jnp.float32)
    return x / (1.0 + jnp.exp(-x))


def sender_of(move):
    me = lax.axis_index("rep")
    return lax.rem(me + (FAR if move < 2 else N_REP - 1), N_REP)


def comes_to(move, target_ref, count_ref):
    sender = sender_of(move)
    return count_ref[sender] > move, lax.rem(target_ref[move, sender], SLOTS_DEV)


def slot_flags(slot, alive_ref, source_ref, target_ref, count_ref):
    me = lax.axis_index("rep")
    leaves = False
    arrives = []
    for move in range(MOVE):
        leaves |= (count_ref[me] > move) & (source_ref[move, me] == slot)
        valid, at = comes_to(move, target_ref, count_ref)
        arrives.append(valid & (at == slot))
    return (alive_ref[slot] == 1) & jnp.logical_not(leaves), arrives


def split(x):
    high = x.astype(jnp.bfloat16)
    return high, (x - high.astype(jnp.float32)).astype(jnp.bfloat16)


def dot(a, b, dims):
    return lax.dot_general(a, b, (dims, ((), ())), preferred_element_type=jnp.float32)


def read_out(query, state):
    rows = jnp.concatenate(split(query), axis=0)
    high, low = split(state)
    by_high = dot(rows, high, ((1,), (0,)))
    by_low = dot(rows, low, ((1,), (0,)))
    return by_high[:STEPS] + by_high[STEPS:] + by_low[:STEPS]


def later_by(x, gap):
    return x if gap == 0 else jnp.concatenate([jnp.zeros((gap, x.shape[1]), x.dtype), x[:-gap]], axis=0)


def head_slice(head):
    return slice(head * DK, (head + 1) * DK)


def ask_kernel(target_ref, count_ref, query_ref, out_ref):
    for move in range(2):
        _, slot = comes_to(move, target_ref, count_ref)
        out_ref[move] = silu(query_ref[slot])


def outbox_kernel(source_ref, states_ref, asked_ref, far_ref, near_ref, sems):
    del asked_ref
    me = lax.axis_index("rep")
    copies = []
    for move in range(MOVE):
        out = far_ref.at[move] if move < 2 else near_ref.at[0]
        copies.append(pltpu.make_async_copy(states_ref.at[source_ref[move, me]], out, sems.at[move]))
    for copy in copies:
        copy.start()
    for copy in copies:
        copy.wait()


def answer_kernel(query_ref, far_ref, out_ref):
    for move in range(2):
        for head in range(HEADS_DEV):
            out_ref[move, :, head_slice(head)] = read_out(query_ref[move, :, head_slice(head)], far_ref[move, head])


def main_kernel(
    alive_ref, source_ref, target_ref, count_ref, rate_ref, query_ref, key_ref, value_ref, states_ref,
    out_ref, new_ref, flag_ref, fade_ref, added_ref, near_query_ref,
):
    step = pl.program_id(0)
    times = lax.broadcasted_iota(jnp.int32, (STEPS, DK), 0).astype(jnp.float32)

    @pl.when(step == 0)
    def _():
        for head in range(HEADS_DEV):
            fade_ref[:, head_slice(head)] = jnp.exp(-rate_ref[head] * (times + 1.0))
        _, slot = comes_to(2, target_ref, count_ref)
        near_query_ref[...] = silu(query_ref[slot])

    for place in range(BLOCK):
        slot = step * BLOCK + place
        stays, arrives = slot_flags(slot, alive_ref, source_ref, target_ref, count_ref)
        live = (stays | arrives[0] | arrives[1] | arrives[2]).astype(jnp.float32)
        for move in range(MOVE):
            flag_ref[move, slot] = jnp.full((STEPS, DK), arrives[move].astype(jnp.float32))
        flag_ref[MOVE, slot] = jnp.full((STEPS, DK), live)
        stays = stays.astype(jnp.float32)
        queries, keys, values = silu(query_ref[slot]), silu(key_ref[slot]), silu(value_ref[slot])
        inside = [jnp.zeros((STEPS, DK), jnp.float32)] * HEADS_DEV
        for gap in range(STEPS):
            older_keys, older_values = later_by(keys, gap), later_by(values, gap)
            for head in range(HEADS_DEV):
                at = head_slice(head)
                inner = jnp.sum(queries[:, at] * older_keys[:, at], axis=1, keepdims=True)
                inside[head] += inner * (older_values[:, at] * jnp.exp(-rate_ref[head] * jnp.full((STEPS, DK), float(gap))))
        for head in range(HEADS_DEV):
            rate = rate_ref[head]
            query, key, value = (x[:, head_slice(head)] for x in (queries, keys, values))
            state = states_ref[place, head]
            out_ref[slot, :, head_slice(head)] = inside[head] + read_out(query, state) * (stays * jnp.exp(-rate * (times + 1.0)))
            value_high, value_low = split(value)
            faded_high, faded_low = split(key * jnp.exp(-rate * (STEPS - 1.0 - times)))
            added = dot(
                jnp.concatenate([faded_high, faded_low, faded_high], axis=0),
                jnp.concatenate([value_high, value_high, value_low], axis=0), ((0,), (0,)))
            fade = jnp.exp(jnp.full((8, DK), -STEPS * rate, jnp.float32))[:1]
            new_ref[place, head] = state * (fade * stays) + added * live
        for move in range(MOVE):
            @pl.when(arrives[move])
            def _(move=move, place=place):
                added_ref[move] = new_ref[place]


def combine_kernel(answer_ref, near_ref, near_query_ref, part_ref, flag_ref, fade_ref, far_in_ref, out_ref, square_ref, far_ref):
    del far_in_ref, far_ref
    moved = [answer_ref[0], answer_ref[1], jnp.concatenate(
        [read_out(near_query_ref[:, head_slice(head)], near_ref[0, head]) for head in range(HEADS_DEV)], axis=1)]
    moved = [x * fade_ref[...] for x in moved]
    for slot in range(SLOTS_DEV):
        total = jnp.zeros((STEPS, DK), jnp.float32)
        for head in range(HEADS_DEV):
            at = head_slice(head)
            row = part_ref[slot, :, at]
            for move in range(MOVE):
                row = jnp.where(flag_ref[move, slot] > 0.0, row + moved[move][:, at], row)
            out_ref[slot, :, at] = row
            total += row * row
        square_ref[slot] = total


def final_kernel(
    target_ref, count_ref, gain_ref, gate_ref, out_ref, square_a_ref, square_b_ref, flag_ref, fade_ref, added_ref, far_ref, near_ref, old_ref,
    attended_ref, new_ref, rows_ref, sems,
):
    del old_ref
    copies = []
    for move in range(MOVE):
        valid, slot = comes_to(move, target_ref, count_ref)
        copies.append((valid, pltpu.make_async_copy(rows_ref.at[move], new_ref.at[slot], sems.at[move])))
        for head in range(HEADS_DEV):
            came = far_ref[move, head] if move < 2 else near_ref[0, head]
            rows_ref[move, head] = came * fade_ref[STEPS - 1:, head_slice(head)] + added_ref[move, head]

        @pl.when(valid)
        def _(copy=copies[-1][1]):
            copy.start()

    for slot in range(SLOTS_DEV):
        total = jnp.sum(square_a_ref[slot] + square_b_ref[slot], axis=1, keepdims=True)
        scale = lax.rsqrt(total * (1.0 / (HEADS * DK)) + epsilon) * flag_ref[MOVE, slot]
        gate = gate_ref[slot].astype(jnp.float32)
        row = out_ref[slot] * gain_ref[...] / (1.0 + jnp.exp(-gate))
        attended_ref[slot] = (row * jnp.concatenate([scale] * HEADS_DEV, axis=1)).astype(jnp.bfloat16)
    for valid, copy in copies:
        @pl.when(valid)
        def _(copy=copy):
            copy.wait()


def call(kernel, outs, in_specs, args, cost=100_000, limit=8, **more):
    return pl.pallas_call(
        kernel, out_shape=outs, in_specs=in_specs,
        compiler_params=pltpu.CompilerParams(vmem_limit_bytes=limit * 1024 * 1024),
        cost_estimate=pl.CostEstimate(flops=cost, bytes_accessed=cost, transcendentals=0), **more,
    )(*args)


def f32(*shape):
    return jax.ShapeDtypeStruct(shape, jnp.float32)


def over_rep(x, distance):
    return lax.ppermute(x, "rep", [(i, (i + distance) % N_REP) for i in range(N_REP)])


def over_head(x, flip):
    return lax.ppermute(x, "head", [(i, i ^ flip) for i in range(N_HEAD)])


def whole(*shape):
    return pl.BlockSpec(shape, lambda i: (0,) * len(shape))


def by_slot(*row):
    return pl.BlockSpec((BLOCK, *row), lambda i: (i, 0, 0, 0))


def run_main(*args):
    row = (HEADS_DEV, DK, DK)
    features = (SLOTS_DEV, STEPS, WIDTH)
    return call(
        main_kernel,
        (f32(*features), f32(SLOTS_DEV, *row), f32(MOVE + 1, SLOTS_DEV, STEPS, DK), f32(STEPS, WIDTH), f32(MOVE, *row), f32(STEPS, WIDTH)),
        [SMEM] * 5 + [whole(*features)] * 3 + [by_slot(*row)], args,
        out_specs=(
            whole(*features), by_slot(*row), whole(MOVE + 1, SLOTS_DEV, STEPS, DK), whole(STEPS, WIDTH), whole(MOVE, *row), whole(STEPS, WIDTH)),
        grid=(SLOTS_DEV // BLOCK,), cost=40_000_000)


def local(states, alive_flag, plan_source, plan_target, move_count, query_proj, key_proj, value_proj, gate_proj, decay_rate, norm_gain):
    row = (HEADS_DEV, DK, DK)
    features = (SLOTS_DEV, STEPS, WIDTH)
    source, target = plan_source.T, plan_target.T
    asked = call(ask_kernel, f32(2, STEPS, WIDTH), [SMEM, SMEM, VMEM], (target, move_count, query_proj), out_specs=VMEM, limit=60)
    far, near = call(
        outbox_kernel, (f32(2, *row), f32(1, *row)), [SMEM, ANY, ANY], (source, states, asked), out_specs=(VMEM, VMEM),
        scratch_shapes=[pltpu.SemaphoreType.DMA((MOVE,))])
    asked = over_rep(asked, FAR)
    near = over_rep(near, 1)
    answer = call(answer_kernel, f32(2, STEPS, WIDTH), [VMEM, VMEM], (asked, far), out_specs=VMEM)
    part, new_states, flags, fade, added, near_query = run_main(
        alive_flag, source, target, move_count, decay_rate, query_proj, key_proj, value_proj, states)
    answer = over_rep(answer, FAR)
    out, square, far = call(
        combine_kernel, (f32(*features), f32(SLOTS_DEV, STEPS, DK), f32(2, *row)), [VMEM] * 6 + [ANY],
        (answer, near, near_query, part, flags, fade, far), out_specs=(VMEM, VMEM, ANY), input_output_aliases={6: 2})
    far = over_rep(far, FAR)
    square = square + over_head(square, 1)
    square = square + over_head(square, 2)
    other = over_head(square, 6)
    return call(
        final_kernel, (jax.ShapeDtypeStruct(features, jnp.bfloat16), f32(SLOTS_DEV, *row)), [SMEM] * 2 + [VMEM] * 10 + [ANY],
        (target, move_count, norm_gain.reshape(1, WIDTH), gate_proj, out, square, other, flags, fade, added, far, near, new_states),
        out_specs=(VMEM, ANY), input_output_aliases={12: 1},
        scratch_shapes=[pltpu.VMEM((MOVE, *row), jnp.float32), pltpu.SemaphoreType.DMA((MOVE,))])


def solution(mesh):
    return jax.shard_map(
        local,
        mesh=mesh,
        in_specs=(
            P("rep", "head", None, None),
            P("rep"),
            P(),
            P(),
            P(),
            P("rep", None, "head"),
            P("rep", None, "head"),
            P("rep", None, "head"),
            P("rep", None, "head"),
            P("head"),
            P("head"),
        ),
        out_specs=(P("rep", None, "head"), P("rep", "head", None, None)),
        check_vma=False,
    )
```

```python
import jax
import jax.numpy as jnp
from jax import lax
from jax.experimental import pallas as pl
from jax.experimental.pallas import tpu as pltpu
from jax.sharding import PartitionSpec as P

SLOTS_DEV = 8
MOVE = 3
STEPS = 4
N_REP = 32
N_HEAD = 8
HEADS = 32
DK = 128
HEADS_DEV = HEADS // N_HEAD
WIDTH = HEADS_DEV * DK
FAR = N_REP // 2
epsilon = 1e-06

HIGHEST = lax.Precision.HIGHEST
VMEM = pl.BlockSpec(memory_space=pltpu.VMEM)
SMEM = pl.BlockSpec(memory_space=pltpu.SMEM)
ANY = pl.BlockSpec(memory_space=pl.ANY)
HBM = pl.BlockSpec(memory_space=pltpu.HBM)
LONG = 10_000_000_000


def silu(x):
    x = x.astype(jnp.float32)
    return x / (1.0 + jnp.exp(-x))


def sender_of(move):
    me = lax.axis_index("rep")
    return lax.rem(me + (FAR if move < 2 else N_REP - 1), N_REP)


SOURCE, VALID, SLOT, STAYS, LIVE, INFO = 0, MOVE, 2 * MOVE, 3 * MOVE, 3 * MOVE + SLOTS_DEV, 3 * MOVE + 2 * SLOTS_DEV


def split(x):
    high = x.astype(jnp.bfloat16)
    return high, (x - high.astype(jnp.float32)).astype(jnp.bfloat16)


def dot(a, b, dims):
    return lax.dot_general(a, b, (dims, ((), ())), preferred_element_type=jnp.float32)


def read_out(query, state):
    rows = jnp.concatenate(split(query), axis=0)
    high, low = split(state)
    by_high = dot(rows, high, ((1,), (0,)))
    by_low = dot(rows, low, ((1,), (0,)))
    return by_high[:STEPS] + by_high[STEPS:] + by_low[:STEPS]


def later_by(x, gap):
    return x if gap == 0 else jnp.concatenate([jnp.zeros((gap, x.shape[1]), x.dtype), x[:-gap]], axis=0)


def head_slice(head):
    return slice(head * DK, (head + 1) * DK)


def times():
    return lax.broadcasted_iota(jnp.int32, (STEPS, DK), 0).astype(jnp.float32)


def ask_kernel(
    alive_ref, source_ref, target_ref, count_ref, rate_ref, query_ref,
    out_ref, near_query_ref, fade_ref, back_ref, info_ref,
):
    me = lax.axis_index("rep")
    for move in range(MOVE):
        sender = sender_of(move)
        slot = lax.rem(target_ref[move, sender], SLOTS_DEV)
        info_ref[SOURCE + move] = source_ref[move, me]
        info_ref[VALID + move] = (count_ref[sender] > move).astype(jnp.int32)
        info_ref[SLOT + move] = slot
        if move < 2:
            out_ref[move] = silu(query_ref[slot])
        else:
            near_query_ref[...] = silu(query_ref[slot])
    for slot in range(SLOTS_DEV):
        stays = alive_ref[slot]
        for move in range(MOVE):
            stays = jnp.where((count_ref[me] > move) & (source_ref[move, me] == slot), 0, stays)
        live = stays
        for move in range(MOVE):
            live = jnp.where((info_ref[VALID + move] == 1) & (info_ref[SLOT + move] == slot), 1, live)
        info_ref[STAYS + slot] = stays
        info_ref[LIVE + slot] = live
    for head in range(HEADS_DEV):
        fade_ref[:, head_slice(head)] = jnp.exp(-rate_ref[head] * (times() + 1.0))
        back_ref[:, head_slice(head)] = jnp.exp(-rate_ref[head] * (STEPS - 1.0 - times()))


def outbox_kernel(info_ref, states_ref, far_ref, near_ref, sems):
    copies = []
    for move in range(MOVE):
        out = far_ref.at[move] if move < 2 else near_ref.at[0]
        copies.append(pltpu.make_async_copy(states_ref.at[info_ref[SOURCE + move]], out, sems.at[move]))
    for copy in copies:
        copy.start()
    for copy in copies:
        copy.wait()


def answer_kernel(query_ref, far_ref, part_ref, out_ref):
    del part_ref
    for move in range(2):
        for head in range(HEADS_DEV):
            out_ref[move, :, head_slice(head)] = read_out(query_ref[move, :, head_slice(head)], far_ref[move, head])


def part_kernel(info_ref, fade_ref, query_ref, key_ref, value_ref, gate_ref, gain_ref, states_ref, out_ref, flag_ref, gate_out_ref):
    for slot in range(SLOTS_DEV):
        for move in range(MOVE):
            arrives = info_ref[VALID + move] * (info_ref[SLOT + move] == slot).astype(jnp.int32)
            flag_ref[move, slot] = jnp.full((STEPS, DK), arrives.astype(jnp.float32))
        live = info_ref[LIVE + slot].astype(jnp.float32)
        stays = info_ref[STAYS + slot].astype(jnp.float32)
        gate_out_ref[slot] = gain_ref[...] * live / (1.0 + jnp.exp(-gate_ref[slot].astype(jnp.float32)))
        queries, keys, values = silu(query_ref[slot]), silu(key_ref[slot]), silu(value_ref[slot])
        inside = [jnp.zeros((STEPS, DK), jnp.float32)] * HEADS_DEV
        for gap in range(STEPS):
            older_keys, older_values = later_by(keys, gap), later_by(values, gap)
            if gap:
                older_values = older_values * fade_ref[gap - 1:gap]
            for head in range(HEADS_DEV):
                at = head_slice(head)
                inside[head] += jnp.sum(queries[:, at] * older_keys[:, at], axis=1, keepdims=True) * older_values[:, at]
        for head in range(HEADS_DEV):
            at = head_slice(head)
            before = read_out(queries[:, at], states_ref[slot, head])
            out_ref[slot, :, at] = inside[head] + before * (fade_ref[:, at] * stays)


def state_kernel(
    info_ref, fade_ref, back_ref, key_ref, value_ref, states_ref, answer_ref, far_in_ref,
    new_ref, added_ref, far_ref, rows_ref, sems,
):
    del answer_ref, far_in_ref, far_ref
    copies = []
    for slot in range(SLOTS_DEV):
        live = info_ref[LIVE + slot].astype(jnp.float32)
        stays = info_ref[STAYS + slot].astype(jnp.float32)
        keys, values = silu(key_ref[slot]) * (back_ref[...] * live), silu(value_ref[slot])
        for head in range(HEADS_DEV):
            at = head_slice(head)
            value_high, value_low = split(values[:, at])
            faded_high, faded_low = split(keys[:, at])
            added = dot(
                jnp.concatenate([faded_high, faded_low, faded_high], axis=0),
                jnp.concatenate([value_high, value_high, value_low], axis=0), ((0,), (0,)))
            rows_ref[slot, head] = states_ref[slot, head] * (fade_ref[STEPS - 1:, at] * stays) + added
        copies.append(pltpu.make_async_copy(rows_ref.at[slot], new_ref.at[slot], sems.at[slot]))
        copies[-1].start()
    for move in range(MOVE):
        @pl.when(info_ref[VALID + move] == 1)
        def _(move=move):
            added_ref[move] = rows_ref[info_ref[SLOT + move]]

    for copy in copies:
        copy.wait()


def combine_kernel(answer_ref, near_ref, near_query_ref, part_ref, flag_ref, fade_ref, added_ref, out_ref, square_ref):
    del added_ref
    moved = [answer_ref[0], answer_ref[1], jnp.concatenate(
        [read_out(near_query_ref[:, head_slice(head)], near_ref[0, head]) for head in range(HEADS_DEV)], axis=1)]
    moved = [x * fade_ref[...] for x in moved]
    for slot in range(SLOTS_DEV):
        total = jnp.zeros((STEPS, DK), jnp.float32)
        for head in range(HEADS_DEV):
            at = head_slice(head)
            row = part_ref[slot, :, at]
            for move in range(MOVE):
                row = jnp.where(flag_ref[move, slot] > 0.0, row + moved[move][:, at], row)
            out_ref[slot, :, at] = row
            total += row * row
        square_ref[slot] = total


def final_kernel(
    info_ref, gate_ref, out_ref, square_a_ref, square_b_ref, fade_ref, added_ref, far_ref, near_ref, old_ref,
    attended_hbm, new_ref, attended_ref, rows_ref, sems,
):
    del old_ref
    copies = []
    for move in range(MOVE):
        valid = info_ref[VALID + move] == 1
        copy = pltpu.make_async_copy(rows_ref.at[move], new_ref.at[info_ref[SLOT + move]], sems.at[move])
        copies.append((valid, copy))
        for head in range(HEADS_DEV):
            came = far_ref[move, head] if move < 2 else near_ref[0, head]
            rows_ref[move, head] = came * fade_ref[STEPS - 1:, head_slice(head)] + added_ref[move, head]

        @pl.when(valid)
        def _(copy=copy):
            copy.start()

    for slot in range(SLOTS_DEV):
        total = jnp.sum(square_a_ref[slot] + square_b_ref[slot], axis=1, keepdims=True)
        scale = lax.rsqrt(total * (1.0 / (HEADS * DK)) + epsilon)
        attended_ref[slot] = (out_ref[slot] * gate_ref[slot] * scale).astype(jnp.bfloat16)
    out_copy = pltpu.make_async_copy(attended_ref, attended_hbm, sems.at[MOVE])
    out_copy.start()
    out_copy.wait()
    for valid, copy in copies:
        @pl.when(valid)
        def _(copy=copy):
            copy.wait()


def call(kernel, outs, in_specs, args, cost=100_000, limit=8, **more):
    return pl.pallas_call(
        kernel, out_shape=outs, in_specs=in_specs,
        compiler_params=pltpu.CompilerParams(vmem_limit_bytes=limit * 1024 * 1024),
        cost_estimate=pl.CostEstimate(flops=cost, bytes_accessed=cost, transcendentals=0), **more,
    )(*args)


def vmem(*shape, dtype=jnp.float32):
    return pltpu.VMEM(shape, dtype)


def in_hbm(*arrays):
    return tuple(pltpu.with_memory_space_constraint(x, pltpu.HBM) for x in arrays)


def over_rep(x, distance):
    return lax.ppermute(x, "rep", [(i, (i + distance) % N_REP) for i in range(N_REP)])


def over_head(x, flip):
    return lax.ppermute(x, "head", [(i, i ^ flip) for i in range(N_HEAD)])


def local(states, alive_flag, plan_source, plan_target, move_count, query_proj, key_proj, value_proj, gate_proj, decay_rate, norm_gain):
    row = (HEADS_DEV, DK, DK)
    features = (SLOTS_DEV, STEPS, WIDTH)
    asked, near_query, fade, back, info = call(
        ask_kernel, (vmem(2, STEPS, WIDTH), vmem(STEPS, WIDTH), vmem(STEPS, WIDTH), vmem(STEPS, WIDTH), pltpu.SMEM((INFO,), jnp.int32)),
        [SMEM] * 5 + [VMEM], in_hbm(alive_flag, plan_source.T, plan_target.T, move_count, decay_rate, query_proj),
        out_specs=(VMEM,) * 4 + (SMEM,))
    asked = over_rep(asked, FAR)
    far, near = call(
        outbox_kernel, (vmem(2, *row), vmem(1, *row)), [SMEM, HBM], (info, *in_hbm(states)), out_specs=(VMEM, VMEM),
        scratch_shapes=[pltpu.SemaphoreType.DMA((MOVE,))], cost=LONG)
    near = over_rep(near, 1)
    part, arrives, gate = call(
        part_kernel, (vmem(*features), vmem(MOVE, SLOTS_DEV, STEPS, DK), vmem(*features)), [SMEM] + [VMEM] * 7,
        (info, fade, query_proj, key_proj, value_proj, gate_proj, norm_gain.reshape(1, WIDTH), states),
        out_specs=(VMEM,) * 3, cost=1_000_000)
    answer = call(answer_kernel, vmem(2, STEPS, WIDTH), [VMEM, VMEM, ANY], (asked, far, part), out_specs=VMEM)
    new_states, added, far = call(
        state_kernel, (pltpu.HBM((SLOTS_DEV, *row), jnp.float32), vmem(MOVE, *row), vmem(2, *row)), [SMEM] + [VMEM] * 5 + [ANY] * 2,
        (info, fade, back, key_proj, value_proj, states, answer, far), out_specs=(HBM, VMEM, VMEM), input_output_aliases={7: 2},
        scratch_shapes=[pltpu.VMEM((SLOTS_DEV, *row), jnp.float32), pltpu.SemaphoreType.DMA((SLOTS_DEV,))], cost=LONG)
    answer = over_rep(answer, FAR)
    far = over_rep(far, FAR)
    out, square = call(
        combine_kernel, (vmem(*features), vmem(SLOTS_DEV, STEPS, DK)), [VMEM] * 6 + [ANY],
        (answer, near, near_query, part, arrives, fade, added), out_specs=(VMEM, VMEM), cost=LONG)
    square = square + over_head(square, 1)
    square = square + over_head(square, 2)
    other = over_head(square, 6)
    return call(
        final_kernel, (jax.ShapeDtypeStruct(features, jnp.bfloat16), jax.ShapeDtypeStruct((SLOTS_DEV, *row), jnp.float32)),
        [SMEM] + [VMEM] * 8 + [ANY], (info, gate, out, square, other, fade, added, far, near, new_states),
        out_specs=(ANY, ANY), input_output_aliases={9: 1},
        scratch_shapes=[
            pltpu.VMEM(features, jnp.bfloat16), pltpu.VMEM((MOVE, *row), jnp.float32), pltpu.SemaphoreType.DMA((MOVE + 1,))])


def solution(mesh):
    return jax.shard_map(
        local,
        mesh=mesh,
        in_specs=(
            P("rep", "head", None, None),
            P("rep"),
            P(),
            P(),
            P(),
            P("rep", None, "head"),
            P("rep", None, "head"),
            P("rep", None, "head"),
            P("rep", None, "head"),
            P("head"),
            P("head"),
        ),
        out_specs=(P("rep", None, "head"), P("rep", "head", None, None)),
        check_vma=False,
    )
```

```python
import jax
import jax.numpy as jnp
from jax import lax
from jax.experimental import pallas as pl
from jax.experimental.pallas import tpu as pltpu
from jax.sharding import PartitionSpec as P

SLOTS_DEV = 8
MOVE = 3
STEPS = 4
N_REP = 32
N_HEAD = 8
HEADS = 32
DK = 128
HEADS_DEV = HEADS // N_HEAD
WIDTH = HEADS_DEV * DK
FAR = N_REP // 2
epsilon = 1e-06

HIGHEST = lax.Precision.HIGHEST
VMEM = pl.BlockSpec(memory_space=pltpu.VMEM)
SMEM = pl.BlockSpec(memory_space=pltpu.SMEM)
ANY = pl.BlockSpec(memory_space=pl.ANY)
HBM = pl.BlockSpec(memory_space=pltpu.HBM)
LONG = 10_000_000_000


def silu(x):
    x = x.astype(jnp.float32)
    return x / (1.0 + jnp.exp(-x))


def sender_of(move):
    me = lax.axis_index("rep")
    return lax.rem(me + (FAR if move < 2 else N_REP - 1), N_REP)


SOURCE, VALID, SLOT, STAYS, LIVE, INFO = 0, MOVE, 2 * MOVE, 3 * MOVE, 3 * MOVE + SLOTS_DEV, 3 * MOVE + 2 * SLOTS_DEV


def split(x):
    high = x.astype(jnp.bfloat16)
    return high, (x - high.astype(jnp.float32)).astype(jnp.bfloat16)


def dot(a, b, dims):
    return lax.dot_general(a, b, (dims, ((), ())), preferred_element_type=jnp.float32)


def read_out(query, state):
    rows = jnp.concatenate(split(query), axis=0)
    high, low = split(state)
    by_high = dot(rows, high, ((1,), (0,)))
    by_low = dot(rows, low, ((1,), (0,)))
    return by_high[:STEPS] + by_high[STEPS:] + by_low[:STEPS]


def later_by(x, gap):
    return x if gap == 0 else jnp.concatenate([jnp.zeros((gap, x.shape[1]), x.dtype), x[:-gap]], axis=0)


def head_slice(head):
    return slice(head * DK, (head + 1) * DK)


def times():
    return lax.broadcasted_iota(jnp.int32, (STEPS, DK), 0).astype(jnp.float32)


def ask_kernel(
    alive_ref, source_ref, target_ref, count_ref, rate_ref, query_ref,
    out_ref, near_query_ref, fade_ref, back_ref, info_ref,
):
    me = lax.axis_index("rep")
    for move in range(MOVE):
        sender = sender_of(move)
        slot = lax.rem(target_ref[move, sender], SLOTS_DEV)
        info_ref[SOURCE + move] = source_ref[move, me]
        info_ref[VALID + move] = (count_ref[sender] > move).astype(jnp.int32)
        info_ref[SLOT + move] = slot
        if move < 2:
            out_ref[move] = silu(query_ref[slot])
        else:
            near_query_ref[...] = silu(query_ref[slot])
    for slot in range(SLOTS_DEV):
        stays = alive_ref[slot]
        for move in range(MOVE):
            stays = jnp.where((count_ref[me] > move) & (source_ref[move, me] == slot), 0, stays)
        live = stays
        for move in range(MOVE):
            live = jnp.where((info_ref[VALID + move] == 1) & (info_ref[SLOT + move] == slot), 1, live)
        info_ref[STAYS + slot] = stays
        info_ref[LIVE + slot] = live
    for head in range(HEADS_DEV):
        fade_ref[:, head_slice(head)] = jnp.exp(-rate_ref[head] * (times() + 1.0))
        back_ref[:, head_slice(head)] = jnp.exp(-rate_ref[head] * (STEPS - 1.0 - times()))


def outbox_kernel(info_ref, states_ref, far_ref, near_ref, sems):
    copies = []
    for move in range(MOVE):
        out = far_ref.at[move] if move < 2 else near_ref.at[0]
        copies.append(pltpu.make_async_copy(states_ref.at[info_ref[SOURCE + move]], out, sems.at[move]))
    for copy in copies:
        copy.start()
    for copy in copies:
        copy.wait()


def answer_kernel(query_ref, far_ref, out_ref):
    for move in range(2):
        for head in range(HEADS_DEV):
            out_ref[move, :, head_slice(head)] = read_out(query_ref[move, :, head_slice(head)], far_ref[move, head])


def part_kernel(
    info_ref, fade_ref, query_ref, key_ref, value_ref, gate_ref, gain_ref, states_ref, answer_ref, far_in_ref,
    out_ref, flag_ref, gate_out_ref, far_ref,
):
    del answer_ref, far_in_ref, far_ref
    for slot in range(SLOTS_DEV):
        for move in range(MOVE):
            arrives = info_ref[VALID + move] * (info_ref[SLOT + move] == slot).astype(jnp.int32)
            flag_ref[move, slot] = jnp.full((STEPS, DK), arrives.astype(jnp.float32))
        live = info_ref[LIVE + slot].astype(jnp.float32)
        stays = info_ref[STAYS + slot].astype(jnp.float32)
        gate_out_ref[slot] = gain_ref[...] * live / (1.0 + jnp.exp(-gate_ref[slot].astype(jnp.float32)))
        queries, keys, values = silu(query_ref[slot]), silu(key_ref[slot]), silu(value_ref[slot])
        inside = [jnp.zeros((STEPS, DK), jnp.float32)] * HEADS_DEV
        for gap in range(STEPS):
            older_keys, older_values = later_by(keys, gap), later_by(values, gap)
            if gap:
                older_values = older_values * fade_ref[gap - 1:gap]
            for head in range(HEADS_DEV):
                at = head_slice(head)
                inside[head] += jnp.sum(queries[:, at] * older_keys[:, at], axis=1, keepdims=True) * older_values[:, at]
        for head in range(HEADS_DEV):
            at = head_slice(head)
            before = read_out(queries[:, at], states_ref[slot, head])
            out_ref[slot, :, at] = inside[head] + before * (fade_ref[:, at] * stays)


def state_kernel(
    info_ref, fade_ref, back_ref, key_ref, value_ref, states_ref, square_ref,
    new_ref, added_ref, rows_ref, sems,
):
    del square_ref
    copies = []
    for slot in range(SLOTS_DEV):
        live = info_ref[LIVE + slot].astype(jnp.float32)
        stays = info_ref[STAYS + slot].astype(jnp.float32)
        keys, values = silu(key_ref[slot]) * (back_ref[...] * live), silu(value_ref[slot])
        for head in range(HEADS_DEV):
            at = head_slice(head)
            value_high, value_low = split(values[:, at])
            faded_high, faded_low = split(keys[:, at])
            added = dot(
                jnp.concatenate([faded_high, faded_low, faded_high], axis=0),
                jnp.concatenate([value_high, value_high, value_low], axis=0), ((0,), (0,)))
            rows_ref[slot, head] = states_ref[slot, head] * (fade_ref[STEPS - 1:, at] * stays) + added
        copies.append(pltpu.make_async_copy(rows_ref.at[slot], new_ref.at[slot], sems.at[slot]))
        copies[-1].start()
    for move in range(MOVE):
        @pl.when(info_ref[VALID + move] == 1)
        def _(move=move):
            added_ref[move] = rows_ref[info_ref[SLOT + move]]

    for copy in copies:
        copy.wait()


def combine_kernel(answer_ref, near_ref, near_query_ref, part_ref, flag_ref, fade_ref, out_ref, square_ref):
    moved = [answer_ref[0], answer_ref[1], jnp.concatenate(
        [read_out(near_query_ref[:, head_slice(head)], near_ref[0, head]) for head in range(HEADS_DEV)], axis=1)]
    moved = [x * fade_ref[...] for x in moved]
    lanes = lax.broadcasted_iota(jnp.int32, (STEPS, DK), 1)
    squares = jnp.zeros((STEPS, DK), jnp.float32)
    for slot in range(SLOTS_DEV):
        total = jnp.zeros((STEPS, DK), jnp.float32)
        for head in range(HEADS_DEV):
            at = head_slice(head)
            row = part_ref[slot, :, at]
            for move in range(MOVE):
                row = jnp.where(flag_ref[move, slot] > 0.0, row + moved[move][:, at], row)
            out_ref[slot, :, at] = row
            total += row * row
        squares = jnp.where(lanes == slot, jnp.sum(total, axis=1, keepdims=True), squares)
    square_ref[...] = squares


def final_kernel(
    info_ref, gate_ref, out_ref, square_a_ref, square_b_ref, fade_ref, added_ref, far_ref, near_ref, old_ref,
    attended_hbm, new_ref, attended_ref, rows_ref, sems,
):
    del old_ref
    copies = []
    for move in range(MOVE):
        valid = info_ref[VALID + move] == 1
        copy = pltpu.make_async_copy(rows_ref.at[move], new_ref.at[info_ref[SLOT + move]], sems.at[move])
        copies.append((valid, copy))
        for head in range(HEADS_DEV):
            came = far_ref[move, head] if move < 2 else near_ref[0, head]
            rows_ref[move, head] = came * fade_ref[STEPS - 1:, head_slice(head)] + added_ref[move, head]

        @pl.when(valid)
        def _(copy=copy):
            copy.start()

    scales = lax.rsqrt((square_a_ref[...] + square_b_ref[...]) * (1.0 / (HEADS * DK)) + epsilon)
    for slot in range(SLOTS_DEV):
        attended_ref[slot] = (out_ref[slot] * gate_ref[slot] * scales[:, slot:slot + 1]).astype(jnp.bfloat16)
    out_copy = pltpu.make_async_copy(attended_ref, attended_hbm, sems.at[MOVE])
    out_copy.start()
    out_copy.wait()
    for valid, copy in copies:
        @pl.when(valid)
        def _(copy=copy):
            copy.wait()


def call(kernel, outs, in_specs, args, cost=100_000, limit=8, **more):
    return pl.pallas_call(
        kernel, out_shape=outs, in_specs=in_specs,
        compiler_params=pltpu.CompilerParams(vmem_limit_bytes=limit * 1024 * 1024),
        cost_estimate=pl.CostEstimate(flops=cost, bytes_accessed=cost, transcendentals=0), **more,
    )(*args)


def vmem(*shape, dtype=jnp.float32):
    return pltpu.VMEM(shape, dtype)


def in_hbm(*arrays):
    return tuple(pltpu.with_memory_space_constraint(x, pltpu.HBM) for x in arrays)


def over_rep(x, distance):
    return lax.ppermute(x, "rep", [(i, (i + distance) % N_REP) for i in range(N_REP)])


def over_head(x, flip):
    return lax.ppermute(x, "head", [(i, i ^ flip) for i in range(N_HEAD)])


def local(states, alive_flag, plan_source, plan_target, move_count, query_proj, key_proj, value_proj, gate_proj, decay_rate, norm_gain):
    row = (HEADS_DEV, DK, DK)
    features = (SLOTS_DEV, STEPS, WIDTH)
    asked, near_query, fade, back, info = call(
        ask_kernel, (vmem(2, STEPS, WIDTH), vmem(STEPS, WIDTH), vmem(STEPS, WIDTH), vmem(STEPS, WIDTH), pltpu.SMEM((INFO,), jnp.int32)),
        [SMEM] * 5 + [VMEM], in_hbm(alive_flag, plan_source.T, plan_target.T, move_count, decay_rate, query_proj),
        out_specs=(VMEM,) * 4 + (SMEM,), cost=LONG)
    asked = over_rep(asked, FAR)
    far, near = call(
        outbox_kernel, (vmem(2, *row), vmem(1, *row)), [SMEM, ANY], (info, states), out_specs=(VMEM, VMEM),
        scratch_shapes=[pltpu.SemaphoreType.DMA((MOVE,))], cost=LONG)
    near = over_rep(near, 1)
    answer = call(answer_kernel, vmem(2, STEPS, WIDTH), [VMEM, VMEM], (asked, far), out_specs=VMEM)
    part, arrives, gate, far = call(
        part_kernel, (vmem(*features), vmem(MOVE, SLOTS_DEV, STEPS, DK), vmem(*features), vmem(2, *row)),
        [SMEM] + [VMEM] * 7 + [ANY] * 2,
        (info, fade, query_proj, key_proj, value_proj, gate_proj, norm_gain.reshape(1, WIDTH), states, answer, far),
        out_specs=(VMEM,) * 4, input_output_aliases={9: 3}, cost=LONG)
    answer = over_rep(answer, FAR)
    far = over_rep(far, FAR)
    out, square = call(
        combine_kernel, (vmem(*features), vmem(STEPS, DK)), [VMEM] * 6,
        (answer, near, near_query, part, arrives, fade), out_specs=(VMEM, VMEM), cost=LONG)
    new_states, added = call(
        state_kernel, (pltpu.HBM((SLOTS_DEV, *row), jnp.float32), vmem(MOVE, *row)), [SMEM] + [VMEM] * 5 + [ANY],
        (info, fade, back, key_proj, value_proj, states, square), out_specs=(HBM, VMEM),
        scratch_shapes=[pltpu.VMEM((SLOTS_DEV, *row), jnp.float32), pltpu.SemaphoreType.DMA((SLOTS_DEV,))], cost=1_000_000)
    square = square + over_head(square, 1)
    square = square + over_head(square, 2)
    other = over_head(square, 6)
    return call(
        final_kernel, (jax.ShapeDtypeStruct(features, jnp.bfloat16), jax.ShapeDtypeStruct((SLOTS_DEV, *row), jnp.float32)),
        [SMEM] + [VMEM] * 8 + [ANY], (info, gate, out, square, other, fade, added, far, near, new_states),
        out_specs=(ANY, ANY), input_output_aliases={9: 1},
        scratch_shapes=[
            pltpu.VMEM(features, jnp.bfloat16), pltpu.VMEM((MOVE, *row), jnp.float32), pltpu.SemaphoreType.DMA((MOVE + 1,))])


def solution(mesh):
    return jax.shard_map(
        local,
        mesh=mesh,
        in_specs=(
            P("rep", "head", None, None),
            P("rep"),
            P(),
            P(),
            P(),
            P("rep", None, "head"),
            P("rep", None, "head"),
            P("rep", None, "head"),
            P("rep", None, "head"),
            P("head"),
            P("head"),
        ),
        out_specs=(P("rep", None, "head"), P("rep", "head", None, None)),
        check_vma=False,
    )
```

```python
import jax
import jax.numpy as jnp
from jax import lax
from jax.experimental import pallas as pl
from jax.experimental.pallas import tpu as pltpu
from jax.sharding import PartitionSpec as P

SLOTS_DEV = 8
MOVE = 3
STEPS = 4
N_REP = 32
N_HEAD = 8
HEADS = 32
DK = 128
HEADS_DEV = HEADS // N_HEAD
WIDTH = HEADS_DEV * DK
FAR = N_REP // 2
epsilon = 1e-06

HIGHEST = lax.Precision.HIGHEST
VMEM = pl.BlockSpec(memory_space=pltpu.VMEM)
SMEM = pl.BlockSpec(memory_space=pltpu.SMEM)
ANY = pl.BlockSpec(memory_space=pl.ANY)
HBM = pl.BlockSpec(memory_space=pltpu.HBM)
LONG = 10_000_000_000


def silu(x):
    x = x.astype(jnp.float32)
    return x / (1.0 + jnp.exp(-x))


def sender_of(move):
    me = lax.axis_index("rep")
    return lax.rem(me + (FAR if move < 2 else N_REP - 1), N_REP)


SOURCE, VALID, SLOT, STAYS, LIVE, INFO = 0, MOVE, 2 * MOVE, 3 * MOVE, 3 * MOVE + SLOTS_DEV, 3 * MOVE + 2 * SLOTS_DEV


def split(x):
    high = x.astype(jnp.bfloat16)
    return high, (x - high.astype(jnp.float32)).astype(jnp.bfloat16)


def dot(a, b, dims):
    return lax.dot_general(a, b, (dims, ((), ())), preferred_element_type=jnp.float32)


def read_out(query, state):
    rows = jnp.concatenate(split(query), axis=0)
    high, low = split(state)
    by_high = dot(rows, high, ((1,), (0,)))
    by_low = dot(rows, low, ((1,), (0,)))
    return by_high[:STEPS] + by_high[STEPS:] + by_low[:STEPS]


def later_by(x, gap):
    return x if gap == 0 else jnp.concatenate([jnp.zeros((gap, x.shape[1]), x.dtype), x[:-gap]], axis=0)


def head_slice(head):
    return slice(head * DK, (head + 1) * DK)


def times():
    return lax.broadcasted_iota(jnp.int32, (STEPS, DK), 0).astype(jnp.float32)


def ask_kernel(
    alive_ref, source_ref, target_ref, count_ref, rate_ref, query_ref,
    out_ref, near_query_ref, fade_ref, back_ref, info_ref,
):
    me = lax.axis_index("rep")
    for move in range(MOVE):
        sender = sender_of(move)
        slot = lax.rem(target_ref[move, sender], SLOTS_DEV)
        info_ref[SOURCE + move] = source_ref[move, me]
        info_ref[VALID + move] = (count_ref[sender] > move).astype(jnp.int32)
        info_ref[SLOT + move] = slot
        if move < 2:
            out_ref[move] = silu(query_ref[slot])
        else:
            near_query_ref[...] = silu(query_ref[slot])
    for slot in range(SLOTS_DEV):
        stays = alive_ref[slot]
        for move in range(MOVE):
            stays = jnp.where((count_ref[me] > move) & (source_ref[move, me] == slot), 0, stays)
        live = stays
        for move in range(MOVE):
            live = jnp.where((info_ref[VALID + move] == 1) & (info_ref[SLOT + move] == slot), 1, live)
        info_ref[STAYS + slot] = stays
        info_ref[LIVE + slot] = live
    for head in range(HEADS_DEV):
        fade_ref[:, head_slice(head)] = jnp.exp(-rate_ref[head] * (times() + 1.0))
        back_ref[:, head_slice(head)] = jnp.exp(-rate_ref[head] * (STEPS - 1.0 - times()))


def outbox_kernel(info_ref, states_ref, far_ref, near_ref, sems):
    copies = []
    for move in range(MOVE):
        out = far_ref.at[move] if move < 2 else near_ref.at[0]
        copies.append(pltpu.make_async_copy(states_ref.at[info_ref[SOURCE + move]], out, sems.at[move]))
    for copy in copies:
        copy.start()
    for copy in copies:
        copy.wait()


def answer_kernel(query_ref, far_ref, out_ref):
    for move in range(2):
        for head in range(HEADS_DEV):
            out_ref[move, :, head_slice(head)] = read_out(query_ref[move, :, head_slice(head)], far_ref[move, head])


def part_kernel(
    info_ref, fade_ref, query_ref, key_ref, value_ref, gate_ref, gain_ref, states_ref, answer_ref, far_in_ref,
    out_ref, flag_ref, gate_out_ref, far_ref,
):
    del answer_ref, far_in_ref, far_ref
    for slot in range(SLOTS_DEV):
        for move in range(MOVE):
            arrives = info_ref[VALID + move] * (info_ref[SLOT + move] == slot).astype(jnp.int32)
            flag_ref[move, slot] = jnp.full((STEPS, DK), arrives.astype(jnp.float32))
        live = info_ref[LIVE + slot].astype(jnp.float32)
        stays = info_ref[STAYS + slot].astype(jnp.float32)
        gate_out_ref[slot] = gain_ref[...] * live / (1.0 + jnp.exp(-gate_ref[slot].astype(jnp.float32)))
        queries, keys, values = silu(query_ref[slot]), silu(key_ref[slot]), silu(value_ref[slot])
        inside = [jnp.zeros((STEPS, DK), jnp.float32)] * HEADS_DEV
        for gap in range(STEPS):
            older_keys, older_values = later_by(keys, gap), later_by(values, gap)
            if gap:
                older_values = older_values * fade_ref[gap - 1:gap]
            for head in range(HEADS_DEV):
                at = head_slice(head)
                inside[head] += jnp.sum(queries[:, at] * older_keys[:, at], axis=1, keepdims=True) * older_values[:, at]
        for head in range(HEADS_DEV):
            at = head_slice(head)
            before = read_out(queries[:, at], states_ref[slot, head])
            out_ref[slot, :, at] = inside[head] + before * (fade_ref[:, at] * stays)


def state_kernel(
    info_ref, fade_ref, back_ref, key_ref, value_ref, states_ref, square_ref,
    new_ref, added_ref, rows_ref, sems,
):
    del square_ref
    copies = []
    for slot in range(SLOTS_DEV):
        live = info_ref[LIVE + slot].astype(jnp.float32)
        stays = info_ref[STAYS + slot].astype(jnp.float32)
        keys, values = silu(key_ref[slot]) * (back_ref[...] * live), silu(value_ref[slot])
        for head in range(HEADS_DEV):
            at = head_slice(head)
            value_high, value_low = split(values[:, at])
            faded_high, faded_low = split(keys[:, at])
            added = dot(
                jnp.concatenate([faded_high, faded_low, faded_high], axis=0),
                jnp.concatenate([value_high, value_high, value_low], axis=0), ((0,), (0,)))
            rows_ref[slot, head] = states_ref[slot, head] * (fade_ref[STEPS - 1:, at] * stays) + added
        copies.append(pltpu.make_async_copy(rows_ref.at[slot], new_ref.at[slot], sems.at[slot]))
        copies[-1].start()
    for move in range(MOVE):
        @pl.when(info_ref[VALID + move] == 1)
        def _(move=move):
            added_ref[move] = rows_ref[info_ref[SLOT + move]]

    for copy in copies:
        copy.wait()


def combine_kernel(answer_ref, near_ref, near_query_ref, part_ref, flag_ref, fade_ref, out_ref, square_ref):
    moved = [answer_ref[0], answer_ref[1], jnp.concatenate(
        [read_out(near_query_ref[:, head_slice(head)], near_ref[0, head]) for head in range(HEADS_DEV)], axis=1)]
    moved = [x * fade_ref[...] for x in moved]
    lanes = lax.broadcasted_iota(jnp.int32, (STEPS, DK), 1)
    squares = jnp.zeros((STEPS, DK), jnp.float32)
    for slot in range(SLOTS_DEV):
        total = jnp.zeros((STEPS, DK), jnp.float32)
        for head in range(HEADS_DEV):
            at = head_slice(head)
            row = part_ref[slot, :, at]
            for move in range(MOVE):
                row = jnp.where(flag_ref[move, slot] > 0.0, row + moved[move][:, at], row)
            out_ref[slot, :, at] = row
            total += row * row
        squares = jnp.where(lanes == slot, jnp.sum(total, axis=1, keepdims=True), squares)
    square_ref[...] = squares


def add_kernel(a_ref, b_ref, added_ref, out_ref):
    del added_ref
    out_ref[...] = a_ref[...] + b_ref[...]


def final_kernel(
    info_ref, gate_ref, out_ref, square_a_ref, square_b_ref, fade_ref, added_ref, far_ref, near_ref, old_ref,
    attended_hbm, new_ref, attended_ref, rows_ref, sems,
):
    del old_ref
    copies = []
    for move in range(MOVE):
        valid = info_ref[VALID + move] == 1
        copy = pltpu.make_async_copy(rows_ref.at[move], new_ref.at[info_ref[SLOT + move]], sems.at[move])
        copies.append((valid, copy))
        for head in range(HEADS_DEV):
            came = far_ref[move, head] if move < 2 else near_ref[0, head]
            rows_ref[move, head] = came * fade_ref[STEPS - 1:, head_slice(head)] + added_ref[move, head]

        @pl.when(valid)
        def _(copy=copy):
            copy.start()

    scales = lax.rsqrt((square_a_ref[...] + square_b_ref[...]) * (1.0 / (HEADS * DK)) + epsilon)
    for slot in range(SLOTS_DEV):
        attended_ref[slot] = (out_ref[slot] * gate_ref[slot] * scales[:, slot:slot + 1]).astype(jnp.bfloat16)
    out_copy = pltpu.make_async_copy(attended_ref, attended_hbm, sems.at[MOVE])
    out_copy.start()
    out_copy.wait()
    for valid, copy in copies:
        @pl.when(valid)
        def _(copy=copy):
            copy.wait()


def call(kernel, outs, in_specs, args, cost=100_000, limit=8, **more):
    return pl.pallas_call(
        kernel, out_shape=outs, in_specs=in_specs,
        compiler_params=pltpu.CompilerParams(vmem_limit_bytes=limit * 1024 * 1024),
        cost_estimate=pl.CostEstimate(flops=cost, bytes_accessed=cost, transcendentals=0), **more,
    )(*args)


def vmem(*shape, dtype=jnp.float32):
    return pltpu.VMEM(shape, dtype)


def in_hbm(*arrays):
    return tuple(pltpu.with_memory_space_constraint(x, pltpu.HBM) for x in arrays)


def over_rep(x, distance):
    return lax.ppermute(x, "rep", [(i, (i + distance) % N_REP) for i in range(N_REP)])


def over_head(x, flip):
    return lax.ppermute(x, "head", [(i, i ^ flip) for i in range(N_HEAD)])


def local(states, alive_flag, plan_source, plan_target, move_count, query_proj, key_proj, value_proj, gate_proj, decay_rate, norm_gain):
    row = (HEADS_DEV, DK, DK)
    features = (SLOTS_DEV, STEPS, WIDTH)
    asked, near_query, fade, back, info = call(
        ask_kernel, (vmem(2, STEPS, WIDTH), vmem(STEPS, WIDTH), vmem(STEPS, WIDTH), vmem(STEPS, WIDTH), pltpu.SMEM((INFO,), jnp.int32)),
        [SMEM] * 5 + [VMEM], in_hbm(alive_flag, plan_source.T, plan_target.T, move_count, decay_rate, query_proj),
        out_specs=(VMEM,) * 4 + (SMEM,), cost=LONG)
    asked = over_rep(asked, FAR)
    far, near = call(
        outbox_kernel, (vmem(2, *row), vmem(1, *row)), [SMEM, ANY], (info, states), out_specs=(VMEM, VMEM),
        scratch_shapes=[pltpu.SemaphoreType.DMA((MOVE,))], cost=LONG)
    near = over_rep(near, 1)
    answer = call(answer_kernel, vmem(2, STEPS, WIDTH), [VMEM, VMEM], (asked, far), out_specs=VMEM)
    part, arrives, gate, far = call(
        part_kernel, (vmem(*features), vmem(MOVE, SLOTS_DEV, STEPS, DK), vmem(*features), vmem(2, *row)),
        [SMEM] + [VMEM] * 7 + [ANY] * 2,
        (info, fade, query_proj, key_proj, value_proj, gate_proj, norm_gain.reshape(1, WIDTH), states, answer, far),
        out_specs=(VMEM,) * 4, input_output_aliases={9: 3}, cost=LONG)
    answer = over_rep(answer, FAR)
    far = over_rep(far, FAR)
    out, square = call(
        combine_kernel, (vmem(*features), vmem(STEPS, DK)), [VMEM] * 6,
        (answer, near, near_query, part, arrives, fade), out_specs=(VMEM, VMEM), cost=LONG)
    new_states, added = call(
        state_kernel, (pltpu.HBM((SLOTS_DEV, *row), jnp.float32), vmem(MOVE, *row)), [SMEM] + [VMEM] * 5 + [ANY],
        (info, fade, back, key_proj, value_proj, states, square), out_specs=(HBM, VMEM),
        scratch_shapes=[pltpu.VMEM((SLOTS_DEV, *row), jnp.float32), pltpu.SemaphoreType.DMA((SLOTS_DEV,))], cost=1_000_000)
    square = square + over_head(square, 1)
    square = call(add_kernel, vmem(STEPS, DK), [VMEM, VMEM, ANY], (square, over_head(square, 2), added), out_specs=VMEM)
    other = over_head(square, 6)
    return call(
        final_kernel, (jax.ShapeDtypeStruct(features, jnp.bfloat16), jax.ShapeDtypeStruct((SLOTS_DEV, *row), jnp.float32)),
        [SMEM] + [VMEM] * 8 + [ANY], (info, gate, out, square, other, fade, added, far, near, new_states),
        out_specs=(ANY, ANY), input_output_aliases={9: 1},
        scratch_shapes=[
            pltpu.VMEM(features, jnp.bfloat16), pltpu.VMEM((MOVE, *row), jnp.float32), pltpu.SemaphoreType.DMA((MOVE + 1,))])


def solution(mesh):
    return jax.shard_map(
        local,
        mesh=mesh,
        in_specs=(
            P("rep", "head", None, None),
            P("rep"),
            P(),
            P(),
            P(),
            P("rep", None, "head"),
            P("rep", None, "head"),
            P("rep", None, "head"),
            P("rep", None, "head"),
            P("head"),
            P("head"),
        ),
        out_specs=(P("rep", None, "head"), P("rep", "head", None, None)),
        check_vma=False,
    )
```

```python
import jax
import jax.numpy as jnp
from jax import lax
from jax.experimental import pallas as pl
from jax.experimental.pallas import tpu as pltpu
from jax.sharding import PartitionSpec as P

SLOTS_DEV = 8
MOVE = 3
STEPS = 4
N_REP = 32
N_HEAD = 8
HEADS = 32
DK = 128
HEADS_DEV = HEADS // N_HEAD
WIDTH = HEADS_DEV * DK
FAR = N_REP // 2
epsilon = 1e-06

HIGHEST = lax.Precision.HIGHEST
VMEM = pl.BlockSpec(memory_space=pltpu.VMEM)
SMEM = pl.BlockSpec(memory_space=pltpu.SMEM)
ANY = pl.BlockSpec(memory_space=pl.ANY)
HBM = pl.BlockSpec(memory_space=pltpu.HBM)
LONG = 10_000_000_000


def silu(x):
    x = x.astype(jnp.float32)
    return x / (1.0 + jnp.exp(-x))


def sender_of(move):
    me = lax.axis_index("rep")
    return lax.rem(me + (FAR if move < 2 else N_REP - 1), N_REP)


SOURCE, VALID, SLOT, STAYS, LIVE, INFO = 0, MOVE, 2 * MOVE, 3 * MOVE, 3 * MOVE + SLOTS_DEV, 3 * MOVE + 2 * SLOTS_DEV


def split(x):
    high = x.astype(jnp.bfloat16)
    return high, (x - high.astype(jnp.float32)).astype(jnp.bfloat16)


def dot(a, b, dims):
    return lax.dot_general(a, b, (dims, ((), ())), preferred_element_type=jnp.float32)


def read_out(query, state):
    rows = jnp.concatenate(split(query), axis=0)
    high, low = split(state)
    by_high = dot(rows, high, ((1,), (0,)))
    by_low = dot(rows, low, ((1,), (0,)))
    return by_high[:STEPS] + by_high[STEPS:] + by_low[:STEPS]


def later_by(x, gap):
    return x if gap == 0 else jnp.concatenate([jnp.zeros((gap, x.shape[1]), x.dtype), x[:-gap]], axis=0)


def head_slice(head):
    return slice(head * DK, (head + 1) * DK)


def times():
    return lax.broadcasted_iota(jnp.int32, (STEPS, DK), 0).astype(jnp.float32)


def ask_kernel(
    alive_ref, source_ref, target_ref, count_ref, rate_ref, query_ref,
    out_ref, near_query_ref, fade_ref, back_ref, info_ref,
):
    me = lax.axis_index("rep")
    for move in range(MOVE):
        sender = sender_of(move)
        slot = lax.rem(target_ref[move, sender], SLOTS_DEV)
        info_ref[SOURCE + move] = source_ref[move, me]
        info_ref[VALID + move] = (count_ref[sender] > move).astype(jnp.int32)
        info_ref[SLOT + move] = slot
        if move < 2:
            out_ref[move] = silu(query_ref[slot])
        else:
            near_query_ref[...] = silu(query_ref[slot])
    for slot in range(SLOTS_DEV):
        stays = alive_ref[slot]
        for move in range(MOVE):
            stays = jnp.where((count_ref[me] > move) & (source_ref[move, me] == slot), 0, stays)
        live = stays
        for move in range(MOVE):
            live = jnp.where((info_ref[VALID + move] == 1) & (info_ref[SLOT + move] == slot), 1, live)
        info_ref[STAYS + slot] = stays
        info_ref[LIVE + slot] = live
    for head in range(HEADS_DEV):
        fade_ref[:, head_slice(head)] = jnp.exp(-rate_ref[head] * (times() + 1.0))
        back_ref[:, head_slice(head)] = jnp.exp(-rate_ref[head] * (STEPS - 1.0 - times()))


def outbox_kernel(info_ref, states_ref, far_ref, near_ref, sems):
    copies = []
    for move in range(MOVE):
        out = far_ref.at[move] if move < 2 else near_ref.at[0]
        copies.append(pltpu.make_async_copy(states_ref.at[info_ref[SOURCE + move]], out, sems.at[move]))
    for copy in copies:
        copy.start()
    for copy in copies:
        copy.wait()


def answer_kernel(query_ref, far_ref, out_ref):
    for move in range(2):
        for head in range(HEADS_DEV):
            out_ref[move, :, head_slice(head)] = read_out(query_ref[move, :, head_slice(head)], far_ref[move, head])


def part_kernel(
    info_ref, fade_ref, query_ref, key_ref, value_ref, gate_ref, gain_ref, states_ref, answer_ref, far_in_ref,
    out_ref, flag_ref, gate_out_ref, far_ref,
):
    del answer_ref, far_in_ref, far_ref
    for slot in range(SLOTS_DEV):
        for move in range(MOVE):
            arrives = info_ref[VALID + move] * (info_ref[SLOT + move] == slot).astype(jnp.int32)
            flag_ref[move, slot] = jnp.full((STEPS, DK), arrives.astype(jnp.float32))
        live = info_ref[LIVE + slot].astype(jnp.float32)
        stays = info_ref[STAYS + slot].astype(jnp.float32)
        gate_out_ref[slot] = gain_ref[...] * live / (1.0 + jnp.exp(-gate_ref[slot].astype(jnp.float32)))
        queries, keys, values = silu(query_ref[slot]), silu(key_ref[slot]), silu(value_ref[slot])
        inside = [jnp.zeros((STEPS, DK), jnp.float32)] * HEADS_DEV
        for gap in range(STEPS):
            older_keys, older_values = later_by(keys, gap), later_by(values, gap)
            if gap:
                older_values = older_values * fade_ref[gap - 1:gap]
            for head in range(HEADS_DEV):
                at = head_slice(head)
                inside[head] += jnp.sum(queries[:, at] * older_keys[:, at], axis=1, keepdims=True) * older_values[:, at]
        for head in range(HEADS_DEV):
            at = head_slice(head)
            before = read_out(queries[:, at], states_ref[slot, head])
            out_ref[slot, :, at] = inside[head] + before * (fade_ref[:, at] * stays)


def state_kernel(
    info_ref, fade_ref, back_ref, key_ref, value_ref, states_ref, square_ref,
    new_ref, added_ref, rows_ref, sems,
):
    del square_ref
    copies = []
    for slot in range(SLOTS_DEV):
        live = info_ref[LIVE + slot].astype(jnp.float32)
        stays = info_ref[STAYS + slot].astype(jnp.float32)
        keys, values = silu(key_ref[slot]) * (back_ref[...] * live), silu(value_ref[slot])
        for head in range(HEADS_DEV):
            at = head_slice(head)
            value_high, value_low = split(values[:, at])
            faded_high, faded_low = split(keys[:, at])
            added = dot(
                jnp.concatenate([faded_high, faded_low, faded_high], axis=0),
                jnp.concatenate([value_high, value_high, value_low], axis=0), ((0,), (0,)))
            rows_ref[slot, head] = states_ref[slot, head] * (fade_ref[STEPS - 1:, at] * stays) + added
        copies.append(pltpu.make_async_copy(rows_ref.at[slot], new_ref.at[slot], sems.at[slot]))
        copies[-1].start()
    for move in range(MOVE):
        @pl.when(info_ref[VALID + move] == 1)
        def _(move=move):
            added_ref[move] = rows_ref[info_ref[SLOT + move]]

    for copy in copies:
        copy.wait()


def combine_kernel(answer_ref, near_ref, near_query_ref, part_ref, flag_ref, fade_ref, out_ref, square_ref):
    moved = [answer_ref[0], answer_ref[1], jnp.concatenate(
        [read_out(near_query_ref[:, head_slice(head)], near_ref[0, head]) for head in range(HEADS_DEV)], axis=1)]
    moved = [x * fade_ref[...] for x in moved]
    lanes = lax.broadcasted_iota(jnp.int32, (STEPS, DK), 1)
    squares = jnp.zeros((STEPS, DK), jnp.float32)
    for slot in range(SLOTS_DEV):
        total = jnp.zeros((STEPS, DK), jnp.float32)
        for head in range(HEADS_DEV):
            at = head_slice(head)
            row = part_ref[slot, :, at]
            for move in range(MOVE):
                row = jnp.where(flag_ref[move, slot] > 0.0, row + moved[move][:, at], row)
            out_ref[slot, :, at] = row
            total += row * row
        squares = jnp.where(lanes == slot, jnp.sum(total, axis=1, keepdims=True), squares)
    square_ref[...] = squares


def add_kernel(a_ref, b_ref, added_ref, out_ref):
    del added_ref
    out_ref[...] = a_ref[...] + b_ref[...]


def update_kernel(info_ref, fade_ref, added_ref, far_ref, near_ref, old_ref, new_ref, rows_ref, sems):
    del old_ref
    copies = []
    for move in range(MOVE):
        valid = info_ref[VALID + move] == 1
        copy = pltpu.make_async_copy(rows_ref.at[move], new_ref.at[info_ref[SLOT + move]], sems.at[move])
        copies.append((valid, copy))
        for head in range(HEADS_DEV):
            came = far_ref[move, head] if move < 2 else near_ref[0, head]
            rows_ref[move, head] = came * fade_ref[STEPS - 1:, head_slice(head)] + added_ref[move, head]

        @pl.when(valid)
        def _(copy=copy):
            copy.start()

    for valid, copy in copies:
        @pl.when(valid)
        def _(copy=copy):
            copy.wait()


def final_kernel(gate_ref, out_ref, square_a_ref, square_b_ref, new_ref, attended_ref):
    del new_ref
    scales = lax.rsqrt((square_a_ref[...] + square_b_ref[...]) * (1.0 / (HEADS * DK)) + epsilon)
    for slot in range(SLOTS_DEV):
        attended_ref[slot] = (out_ref[slot] * gate_ref[slot] * scales[:, slot:slot + 1]).astype(jnp.bfloat16)


def call(kernel, outs, in_specs, args, cost=100_000, limit=8, **more):
    return pl.pallas_call(
        kernel, out_shape=outs, in_specs=in_specs,
        compiler_params=pltpu.CompilerParams(vmem_limit_bytes=limit * 1024 * 1024),
        cost_estimate=pl.CostEstimate(flops=cost, bytes_accessed=cost, transcendentals=0), **more,
    )(*args)


def vmem(*shape, dtype=jnp.float32):
    return pltpu.VMEM(shape, dtype)


def in_hbm(*arrays):
    return tuple(pltpu.with_memory_space_constraint(x, pltpu.HBM) for x in arrays)


def over_rep(x, distance):
    return lax.ppermute(x, "rep", [(i, (i + distance) % N_REP) for i in range(N_REP)])


def over_head(x, flip):
    return lax.ppermute(x, "head", [(i, i ^ flip) for i in range(N_HEAD)])


def local(states, alive_flag, plan_source, plan_target, move_count, query_proj, key_proj, value_proj, gate_proj, decay_rate, norm_gain):
    row = (HEADS_DEV, DK, DK)
    features = (SLOTS_DEV, STEPS, WIDTH)
    asked, near_query, fade, back, info = call(
        ask_kernel, (vmem(2, STEPS, WIDTH), vmem(STEPS, WIDTH), vmem(STEPS, WIDTH), vmem(STEPS, WIDTH), pltpu.SMEM((INFO,), jnp.int32)),
        [SMEM] * 5 + [VMEM], in_hbm(alive_flag, plan_source.T, plan_target.T, move_count, decay_rate, query_proj),
        out_specs=(VMEM,) * 4 + (SMEM,), cost=LONG)
    asked = over_rep(asked, FAR)
    far, near = call(
        outbox_kernel, (vmem(2, *row), vmem(1, *row)), [SMEM, ANY], (info, states), out_specs=(VMEM, VMEM),
        scratch_shapes=[pltpu.SemaphoreType.DMA((MOVE,))], cost=LONG)
    near = over_rep(near, 1)
    answer = call(answer_kernel, vmem(2, STEPS, WIDTH), [VMEM, VMEM], (asked, far), out_specs=VMEM)
    part, arrives, gate, far = call(
        part_kernel, (vmem(*features), vmem(MOVE, SLOTS_DEV, STEPS, DK), vmem(*features), vmem(2, *row)),
        [SMEM] + [VMEM] * 7 + [ANY] * 2,
        (info, fade, query_proj, key_proj, value_proj, gate_proj, norm_gain.reshape(1, WIDTH), states, answer, far),
        out_specs=(VMEM,) * 4, input_output_aliases={9: 3}, cost=LONG)
    answer = over_rep(answer, FAR)
    far = over_rep(far, FAR)
    out, square = call(
        combine_kernel, (vmem(*features), vmem(STEPS, DK)), [VMEM] * 6,
        (answer, near, near_query, part, arrives, fade), out_specs=(VMEM, VMEM), cost=LONG)
    new_states, added = call(
        state_kernel, (pltpu.HBM((SLOTS_DEV, *row), jnp.float32), vmem(MOVE, *row)), [SMEM] + [VMEM] * 5 + [ANY],
        (info, fade, back, key_proj, value_proj, states, square), out_specs=(HBM, VMEM),
        scratch_shapes=[pltpu.VMEM((SLOTS_DEV, *row), jnp.float32), pltpu.SemaphoreType.DMA((SLOTS_DEV,))], cost=1_000_000)
    square = square + over_head(square, 1)
    square = call(add_kernel, vmem(STEPS, DK), [VMEM, VMEM, ANY], (square, over_head(square, 2), added), out_specs=VMEM)
    other = over_head(square, 6)
    new_states = call(
        update_kernel, jax.ShapeDtypeStruct((SLOTS_DEV, *row), jnp.float32), [SMEM] + [VMEM] * 4 + [ANY],
        (info, fade, added, far, near, new_states), out_specs=ANY, input_output_aliases={5: 0},
        scratch_shapes=[pltpu.VMEM((MOVE, *row), jnp.float32), pltpu.SemaphoreType.DMA((MOVE,))], cost=100_000)
    attended = call(
        final_kernel, jax.ShapeDtypeStruct(features, jnp.bfloat16), [VMEM] * 4 + [HBM], (gate, out, square, other, *in_hbm(new_states)),
        out_specs=VMEM)
    return attended, new_states


def solution(mesh):
    return jax.shard_map(
        local,
        mesh=mesh,
        in_specs=(
            P("rep", "head", None, None),
            P("rep"),
            P(),
            P(),
            P(),
            P("rep", None, "head"),
            P("rep", None, "head"),
            P("rep", None, "head"),
            P("rep", None, "head"),
            P("head"),
            P("head"),
        ),
        out_specs=(P("rep", None, "head"), P("rep", "head", None, None)),
        check_vma=False,
    )
```

```python
import jax
import jax.numpy as jnp
from jax import lax
from jax.experimental import pallas as pl
from jax.experimental.pallas import tpu as pltpu
from jax.sharding import PartitionSpec as P

SLOTS_DEV = 8
MOVE = 3
STEPS = 4
N_REP = 32
N_HEAD = 8
HEADS = 32
DK = 128
HEADS_DEV = HEADS // N_HEAD
WIDTH = HEADS_DEV * DK
FAR = N_REP // 2
epsilon = 1e-06

HIGHEST = lax.Precision.HIGHEST
VMEM = pl.BlockSpec(memory_space=pltpu.VMEM)
SMEM = pl.BlockSpec(memory_space=pltpu.SMEM)
ANY = pl.BlockSpec(memory_space=pl.ANY)
HBM = pl.BlockSpec(memory_space=pltpu.HBM)
LONG = 10_000_000_000


def silu(x):
    x = x.astype(jnp.float32)
    return x / (1.0 + jnp.exp(-x))


def sender_of(move):
    me = lax.axis_index("rep")
    return lax.rem(me + (FAR if move < 2 else N_REP - 1), N_REP)


SOURCE, VALID, SLOT, INFO = 0, MOVE, 2 * MOVE, 3 * MOVE
STAYS, LIVE, ROWS = 0, SLOTS_DEV, 2 * SLOTS_DEV


def split(x):
    high = x.astype(jnp.bfloat16)
    return high, (x - high.astype(jnp.float32)).astype(jnp.bfloat16)


def dot(a, b, dims):
    return lax.dot_general(a, b, (dims, ((), ())), preferred_element_type=jnp.float32)


def read_out(query, state):
    rows = jnp.concatenate(split(query), axis=0)
    high, low = split(state)
    by_high = dot(rows, high, ((1,), (0,)))
    by_low = dot(rows, low, ((1,), (0,)))
    return by_high[:STEPS] + by_high[STEPS:] + by_low[:STEPS]


def later_by(x, gap):
    return x if gap == 0 else jnp.concatenate([jnp.zeros((gap, x.shape[1]), x.dtype), x[:-gap]], axis=0)


def head_slice(head):
    return slice(head * DK, (head + 1) * DK)


def times():
    return lax.broadcasted_iota(jnp.int32, (STEPS, DK), 0).astype(jnp.float32)


def ask_kernel(source_ref, target_ref, count_ref, query_ref, out_ref, info_ref):
    me = lax.axis_index("rep")
    for move in range(MOVE):
        sender = sender_of(move)
        slot = lax.rem(target_ref[move, sender], SLOTS_DEV)
        if move < 2:
            out_ref[move] = silu(query_ref[slot])
        info_ref[SOURCE + move] = source_ref[move, me]
        info_ref[VALID + move] = (count_ref[sender] > move).astype(jnp.int32)
        info_ref[SLOT + move] = slot


def prepare_kernel(alive_ref, count_ref, rate_ref, info_ref, query_ref, rows_ref, near_query_ref, fade_ref, back_ref):
    count = count_ref[lax.axis_index("rep")]
    near_query_ref[...] = silu(query_ref[info_ref[SLOT + 2]])
    for slot in range(SLOTS_DEV):
        stays = alive_ref[slot]
        for move in range(MOVE):
            stays = jnp.where((count > move) & (info_ref[SOURCE + move] == slot), 0, stays)
        live = stays
        for move in range(MOVE):
            live = jnp.where((info_ref[VALID + move] == 1) & (info_ref[SLOT + move] == slot), 1, live)
        rows_ref[STAYS + slot] = stays
        rows_ref[LIVE + slot] = live
    for head in range(HEADS_DEV):
        fade_ref[:, head_slice(head)] = jnp.exp(-rate_ref[head] * (times() + 1.0))
        back_ref[:, head_slice(head)] = jnp.exp(-rate_ref[head] * (STEPS - 1.0 - times()))


def outbox_kernel(info_ref, states_ref, far_ref, near_ref, sems):
    copies = []
    for move in range(MOVE):
        out = far_ref.at[move] if move < 2 else near_ref.at[0]
        copies.append(pltpu.make_async_copy(states_ref.at[info_ref[SOURCE + move]], out, sems.at[move]))
    for copy in copies:
        copy.start()
    for copy in copies:
        copy.wait()


def answer_kernel(query_ref, far_ref, fade_ref, out_ref):
    del fade_ref
    for move in range(2):
        for head in range(HEADS_DEV):
            out_ref[move, :, head_slice(head)] = read_out(query_ref[move, :, head_slice(head)], far_ref[move, head])


def part_kernel(
    info_ref, flags_ref, fade_ref, query_ref, key_ref, value_ref, gate_ref, gain_ref, states_ref, answer_ref, far_in_ref,
    out_ref, flag_ref, gate_out_ref, far_ref,
):
    del answer_ref, far_in_ref, far_ref
    for slot in range(SLOTS_DEV):
        for move in range(MOVE):
            arrives = info_ref[VALID + move] * (info_ref[SLOT + move] == slot).astype(jnp.int32)
            flag_ref[move, slot] = jnp.full((STEPS, DK), arrives.astype(jnp.float32))
        live = flags_ref[LIVE + slot].astype(jnp.float32)
        stays = flags_ref[STAYS + slot].astype(jnp.float32)
        gate_out_ref[slot] = gain_ref[...] * live / (1.0 + jnp.exp(-gate_ref[slot].astype(jnp.float32)))
        queries, keys, values = silu(query_ref[slot]), silu(key_ref[slot]), silu(value_ref[slot])
        inside = [jnp.zeros((STEPS, DK), jnp.float32)] * HEADS_DEV
        for gap in range(STEPS):
            older_keys, older_values = later_by(keys, gap), later_by(values, gap)
            if gap:
                older_values = older_values * fade_ref[gap - 1:gap]
            for head in range(HEADS_DEV):
                at = head_slice(head)
                inside[head] += jnp.sum(queries[:, at] * older_keys[:, at], axis=1, keepdims=True) * older_values[:, at]
        for head in range(HEADS_DEV):
            at = head_slice(head)
            before = read_out(queries[:, at], states_ref[slot, head])
            out_ref[slot, :, at] = inside[head] + before * (fade_ref[:, at] * stays)


def state_kernel(
    info_ref, flags_ref, fade_ref, back_ref, key_ref, value_ref, states_ref, square_ref,
    new_ref, added_ref, rows_ref, sems,
):
    del square_ref
    copies = []
    for slot in range(SLOTS_DEV):
        live = flags_ref[LIVE + slot].astype(jnp.float32)
        stays = flags_ref[STAYS + slot].astype(jnp.float32)
        keys, values = silu(key_ref[slot]) * (back_ref[...] * live), silu(value_ref[slot])
        for head in range(HEADS_DEV):
            at = head_slice(head)
            value_high, value_low = split(values[:, at])
            faded_high, faded_low = split(keys[:, at])
            added = dot(
                jnp.concatenate([faded_high, faded_low, faded_high], axis=0),
                jnp.concatenate([value_high, value_high, value_low], axis=0), ((0,), (0,)))
            rows_ref[slot, head] = states_ref[slot, head] * (fade_ref[STEPS - 1:, at] * stays) + added
        copies.append(pltpu.make_async_copy(rows_ref.at[slot], new_ref.at[slot], sems.at[slot]))
        copies[-1].start()
    for move in range(MOVE):
        @pl.when(info_ref[VALID + move] == 1)
        def _(move=move):
            added_ref[move] = rows_ref[info_ref[SLOT + move]]

    for copy in copies:
        copy.wait()


def combine_kernel(answer_ref, near_ref, near_query_ref, part_ref, flag_ref, fade_ref, out_ref, square_ref):
    moved = [answer_ref[0], answer_ref[1], jnp.concatenate(
        [read_out(near_query_ref[:, head_slice(head)], near_ref[0, head]) for head in range(HEADS_DEV)], axis=1)]
    moved = [x * fade_ref[...] for x in moved]
    lanes = lax.broadcasted_iota(jnp.int32, (STEPS, DK), 1)
    squares = jnp.zeros((STEPS, DK), jnp.float32)
    for slot in range(SLOTS_DEV):
        total = jnp.zeros((STEPS, DK), jnp.float32)
        for head in range(HEADS_DEV):
            at = head_slice(head)
            row = part_ref[slot, :, at]
            for move in range(MOVE):
                row = jnp.where(flag_ref[move, slot] > 0.0, row + moved[move][:, at], row)
            out_ref[slot, :, at] = row
            total += row * row
        squares = jnp.where(lanes == slot, jnp.sum(total, axis=1, keepdims=True), squares)
    square_ref[...] = squares


def add_kernel(a_ref, b_ref, added_ref, out_ref):
    del added_ref
    out_ref[...] = a_ref[...] + b_ref[...]


def update_kernel(info_ref, fade_ref, added_ref, far_ref, near_ref, old_ref, new_ref, rows_ref, sems):
    del old_ref
    copies = []
    for move in range(MOVE):
        valid = info_ref[VALID + move] == 1
        copy = pltpu.make_async_copy(rows_ref.at[move], new_ref.at[info_ref[SLOT + move]], sems.at[move])
        copies.append((valid, copy))
        for head in range(HEADS_DEV):
            came = far_ref[move, head] if move < 2 else near_ref[0, head]
            rows_ref[move, head] = came * fade_ref[STEPS - 1:, head_slice(head)] + added_ref[move, head]

        @pl.when(valid)
        def _(copy=copy):
            copy.start()

    for valid, copy in copies:
        @pl.when(valid)
        def _(copy=copy):
            copy.wait()


def final_kernel(gate_ref, out_ref, square_a_ref, square_b_ref, new_ref, attended_ref):
    del new_ref
    scales = lax.rsqrt((square_a_ref[...] + square_b_ref[...]) * (1.0 / (HEADS * DK)) + epsilon)
    for slot in range(SLOTS_DEV):
        attended_ref[slot] = (out_ref[slot] * gate_ref[slot] * scales[:, slot:slot + 1]).astype(jnp.bfloat16)


def call(kernel, outs, in_specs, args, cost=100_000, limit=8, **more):
    return pl.pallas_call(
        kernel, out_shape=outs, in_specs=in_specs,
        compiler_params=pltpu.CompilerParams(vmem_limit_bytes=limit * 1024 * 1024),
        cost_estimate=pl.CostEstimate(flops=cost, bytes_accessed=cost, transcendentals=0), **more,
    )(*args)


def vmem(*shape, dtype=jnp.float32):
    return pltpu.VMEM(shape, dtype)


def in_hbm(*arrays):
    return tuple(pltpu.with_memory_space_constraint(x, pltpu.HBM) for x in arrays)


def over_rep(x, distance):
    return lax.ppermute(x, "rep", [(i, (i + distance) % N_REP) for i in range(N_REP)])


def over_head(x, flip):
    return lax.ppermute(x, "head", [(i, i ^ flip) for i in range(N_HEAD)])


def local(states, alive_flag, plan_source, plan_target, move_count, query_proj, key_proj, value_proj, gate_proj, decay_rate, norm_gain):
    row = (HEADS_DEV, DK, DK)
    features = (SLOTS_DEV, STEPS, WIDTH)
    source, target = plan_source.T, plan_target.T
    asked, info = call(
        ask_kernel, (vmem(2, STEPS, WIDTH), pltpu.SMEM((INFO,), jnp.int32)), [SMEM] * 3 + [VMEM],
        in_hbm(source, target, move_count, query_proj), out_specs=(VMEM, SMEM), cost=LONG)
    asked = over_rep(asked, FAR)
    far, near = call(
        outbox_kernel, (vmem(2, *row), vmem(1, *row)), [SMEM, ANY], (info, states), out_specs=(VMEM, VMEM),
        scratch_shapes=[pltpu.SemaphoreType.DMA((MOVE,))], cost=LONG)
    near = over_rep(near, 1)
    rows, near_query, fade, back = call(
        prepare_kernel, (pltpu.SMEM((ROWS,), jnp.int32), vmem(STEPS, WIDTH), vmem(STEPS, WIDTH), vmem(STEPS, WIDTH)),
        [SMEM] * 4 + [VMEM], (*in_hbm(alive_flag, move_count, decay_rate), info, query_proj), out_specs=(SMEM,) + (VMEM,) * 3)
    answer = call(answer_kernel, vmem(2, STEPS, WIDTH), [VMEM, VMEM, ANY], (asked, far, fade), out_specs=VMEM)
    part, arrives, gate, far = call(
        part_kernel, (vmem(*features), vmem(MOVE, SLOTS_DEV, STEPS, DK), vmem(*features), vmem(2, *row)),
        [SMEM] * 2 + [VMEM] * 7 + [ANY] * 2,
        (info, rows, fade, query_proj, key_proj, value_proj, gate_proj, norm_gain.reshape(1, WIDTH), states, answer, far),
        out_specs=(VMEM,) * 4, input_output_aliases={10: 3}, cost=LONG)
    answer = over_rep(answer, FAR)
    far = over_rep(far, FAR)
    out, square = call(
        combine_kernel, (vmem(*features), vmem(STEPS, DK)), [VMEM] * 6,
        (answer, near, near_query, part, arrives, fade), out_specs=(VMEM, VMEM), cost=LONG)
    new_states, added = call(
        state_kernel, (pltpu.HBM((SLOTS_DEV, *row), jnp.float32), vmem(MOVE, *row)), [SMEM] * 2 + [VMEM] * 5 + [ANY],
        (info, rows, fade, back, key_proj, value_proj, states, square), out_specs=(HBM, VMEM),
        scratch_shapes=[pltpu.VMEM((SLOTS_DEV, *row), jnp.float32), pltpu.SemaphoreType.DMA((SLOTS_DEV,))], cost=1_000_000)
    square = square + over_head(square, 1)
    square = call(add_kernel, vmem(STEPS, DK), [VMEM, VMEM, ANY], (square, over_head(square, 2), added), out_specs=VMEM)
    other = over_head(square, 6)
    new_states = call(
        update_kernel, jax.ShapeDtypeStruct((SLOTS_DEV, *row), jnp.float32), [SMEM] + [VMEM] * 4 + [ANY],
        (info, fade, added, far, near, new_states), out_specs=ANY, input_output_aliases={5: 0},
        scratch_shapes=[pltpu.VMEM((MOVE, *row), jnp.float32), pltpu.SemaphoreType.DMA((MOVE,))], cost=100_000)
    attended = call(
        final_kernel, jax.ShapeDtypeStruct(features, jnp.bfloat16), [VMEM] * 4 + [HBM], (gate, out, square, other, *in_hbm(new_states)),
        out_specs=VMEM)
    return attended, new_states


def solution(mesh):
    return jax.shard_map(
        local,
        mesh=mesh,
        in_specs=(
            P("rep", "head", None, None),
            P("rep"),
            P(),
            P(),
            P(),
            P("rep", None, "head"),
            P("rep", None, "head"),
            P("rep", None, "head"),
            P("rep", None, "head"),
            P("head"),
            P("head"),
        ),
        out_specs=(P("rep", None, "head"), P("rep", "head", None, None)),
        check_vma=False,
    )
```

```python
import jax
import jax.numpy as jnp
from jax import lax
from jax.experimental import pallas as pl
from jax.experimental.pallas import tpu as pltpu
from jax.sharding import PartitionSpec as P

SLOTS_DEV = 8
MOVE = 3
STEPS = 4
N_REP = 32
N_HEAD = 8
HEADS = 32
DK = 128
HEADS_DEV = HEADS // N_HEAD
WIDTH = HEADS_DEV * DK
FAR = N_REP // 2
epsilon = 1e-06

HIGHEST = lax.Precision.HIGHEST
VMEM = pl.BlockSpec(memory_space=pltpu.VMEM)
SMEM = pl.BlockSpec(memory_space=pltpu.SMEM)
ANY = pl.BlockSpec(memory_space=pl.ANY)
HBM = pl.BlockSpec(memory_space=pltpu.HBM)
LONG = 10_000_000_000


def silu(x):
    x = x.astype(jnp.float32)
    return x / (1.0 + jnp.exp(-x))


def sender_of(move):
    me = lax.axis_index("rep")
    return lax.rem(me + (FAR if move < 2 else N_REP - 1), N_REP)


SOURCE, VALID, SLOT, INFO = 0, MOVE, 2 * MOVE, 3 * MOVE
STAYS, LIVE, ROWS = 0, SLOTS_DEV, 2 * SLOTS_DEV


def split(x):
    high = x.astype(jnp.bfloat16)
    return high, (x - high.astype(jnp.float32)).astype(jnp.bfloat16)


def dot(a, b, dims):
    return lax.dot_general(a, b, (dims, ((), ())), preferred_element_type=jnp.float32)


def read_out(query, state):
    query_high, query_low = split(query)
    rows = jnp.concatenate([
        jnp.concatenate([query_high, query_high], axis=1), jnp.concatenate([query_low, jnp.zeros_like(query_low)], axis=1)], axis=0)
    both = dot(rows, jnp.concatenate(split(state), axis=0), ((1,), (0,)))
    return both[:STEPS] + both[STEPS:]


def later_by(x, gap):
    return x if gap == 0 else jnp.concatenate([jnp.zeros((gap, x.shape[1]), x.dtype), x[:-gap]], axis=0)


def head_slice(head):
    return slice(head * DK, (head + 1) * DK)


def times():
    return lax.broadcasted_iota(jnp.int32, (STEPS, DK), 0).astype(jnp.float32)


def ask_kernel(source_ref, target_ref, count_ref, query_ref, out_ref, info_ref):
    me = lax.axis_index("rep")
    for move in range(MOVE):
        sender = sender_of(move)
        slot = lax.rem(target_ref[move, sender], SLOTS_DEV)
        if move < 2:
            out_ref[move] = silu(query_ref[slot])
        info_ref[SOURCE + move] = source_ref[move, me]
        info_ref[VALID + move] = (count_ref[sender] > move).astype(jnp.int32)
        info_ref[SLOT + move] = slot


def prepare_kernel(alive_ref, count_ref, rate_ref, info_ref, query_ref, rows_ref, near_query_ref, fade_ref, back_ref):
    count = count_ref[lax.axis_index("rep")]
    near_query_ref[...] = silu(query_ref[info_ref[SLOT + 2]])
    for slot in range(SLOTS_DEV):
        stays = alive_ref[slot]
        for move in range(MOVE):
            stays = jnp.where((count > move) & (info_ref[SOURCE + move] == slot), 0, stays)
        live = stays
        for move in range(MOVE):
            live = jnp.where((info_ref[VALID + move] == 1) & (info_ref[SLOT + move] == slot), 1, live)
        rows_ref[STAYS + slot] = stays
        rows_ref[LIVE + slot] = live
    for head in range(HEADS_DEV):
        fade_ref[:, head_slice(head)] = jnp.exp(-rate_ref[head] * (times() + 1.0))
        back_ref[:, head_slice(head)] = jnp.exp(-rate_ref[head] * (STEPS - 1.0 - times()))


def outbox_kernel(info_ref, states_ref, far_ref, near_ref, sems):
    copies = []
    for move in range(MOVE):
        out = far_ref.at[move] if move < 2 else near_ref.at[0]
        copies.append(pltpu.make_async_copy(states_ref.at[info_ref[SOURCE + move]], out, sems.at[move]))
    for copy in copies:
        copy.start()
    for copy in copies:
        copy.wait()


def answer_kernel(query_ref, far_ref, fade_ref, out_ref):
    del fade_ref
    for move in range(2):
        for head in range(HEADS_DEV):
            out_ref[move, :, head_slice(head)] = read_out(query_ref[move, :, head_slice(head)], far_ref[move, head])


def part_kernel(
    info_ref, flags_ref, fade_ref, query_ref, key_ref, value_ref, gate_ref, gain_ref, states_ref, answer_ref, far_in_ref,
    out_ref, flag_ref, gate_out_ref, far_ref,
):
    del answer_ref, far_in_ref, far_ref
    for slot in range(SLOTS_DEV):
        for move in range(MOVE):
            arrives = info_ref[VALID + move] * (info_ref[SLOT + move] == slot).astype(jnp.int32)
            flag_ref[move, slot] = jnp.full((STEPS, DK), arrives.astype(jnp.float32))
        live = flags_ref[LIVE + slot].astype(jnp.float32)
        stays = flags_ref[STAYS + slot].astype(jnp.float32)
        gate_out_ref[slot] = gain_ref[...] * live / (1.0 + jnp.exp(-gate_ref[slot].astype(jnp.float32)))
        queries, keys, values = silu(query_ref[slot]), silu(key_ref[slot]), silu(value_ref[slot])
        inside = [jnp.zeros((STEPS, DK), jnp.float32)] * HEADS_DEV
        for gap in range(STEPS):
            older_keys, older_values = later_by(keys, gap), later_by(values, gap)
            if gap:
                older_values = older_values * fade_ref[gap - 1:gap]
            for head in range(HEADS_DEV):
                at = head_slice(head)
                inside[head] += jnp.sum(queries[:, at] * older_keys[:, at], axis=1, keepdims=True) * older_values[:, at]
        for head in range(HEADS_DEV):
            at = head_slice(head)
            before = read_out(queries[:, at], states_ref[slot, head])
            out_ref[slot, :, at] = inside[head] + before * (fade_ref[:, at] * stays)


def state_kernel(
    info_ref, flags_ref, fade_ref, back_ref, key_ref, value_ref, states_ref, square_ref,
    new_ref, added_ref, rows_ref, sems,
):
    del square_ref
    copies = []
    for slot in range(SLOTS_DEV):
        live = flags_ref[LIVE + slot].astype(jnp.float32)
        stays = flags_ref[STAYS + slot].astype(jnp.float32)
        keys, values = silu(key_ref[slot]) * (back_ref[...] * live), silu(value_ref[slot])
        for head in range(HEADS_DEV):
            at = head_slice(head)
            value_high, value_low = split(values[:, at])
            faded_high, faded_low = split(keys[:, at])
            added = dot(
                jnp.concatenate([faded_high, faded_low, faded_high], axis=0),
                jnp.concatenate([value_high, value_high, value_low], axis=0), ((0,), (0,)))
            rows_ref[slot, head] = states_ref[slot, head] * (fade_ref[STEPS - 1:, at] * stays) + added
        copies.append(pltpu.make_async_copy(rows_ref.at[slot], new_ref.at[slot], sems.at[slot]))
        copies[-1].start()
    for move in range(MOVE):
        @pl.when(info_ref[VALID + move] == 1)
        def _(move=move):
            added_ref[move] = rows_ref[info_ref[SLOT + move]]

    for copy in copies:
        copy.wait()


def combine_kernel(answer_ref, near_ref, near_query_ref, part_ref, flag_ref, fade_ref, out_ref, square_ref):
    moved = [answer_ref[0], answer_ref[1], jnp.concatenate(
        [read_out(near_query_ref[:, head_slice(head)], near_ref[0, head]) for head in range(HEADS_DEV)], axis=1)]
    moved = [x * fade_ref[...] for x in moved]
    lanes = lax.broadcasted_iota(jnp.int32, (STEPS, DK), 1)
    squares = jnp.zeros((STEPS, DK), jnp.float32)
    for slot in range(SLOTS_DEV):
        total = jnp.zeros((STEPS, DK), jnp.float32)
        for head in range(HEADS_DEV):
            at = head_slice(head)
            row = part_ref[slot, :, at]
            for move in range(MOVE):
                row = jnp.where(flag_ref[move, slot] > 0.0, row + moved[move][:, at], row)
            out_ref[slot, :, at] = row
            total += row * row
        squares = jnp.where(lanes == slot, jnp.sum(total, axis=1, keepdims=True), squares)
    square_ref[...] = squares


def add_kernel(a_ref, b_ref, added_ref, out_ref):
    del added_ref
    out_ref[...] = a_ref[...] + b_ref[...]


def update_kernel(info_ref, fade_ref, added_ref, far_ref, near_ref, old_ref, new_ref, rows_ref, sems):
    del old_ref
    copies = []
    for move in range(MOVE):
        valid = info_ref[VALID + move] == 1
        copy = pltpu.make_async_copy(rows_ref.at[move], new_ref.at[info_ref[SLOT + move]], sems.at[move])
        copies.append((valid, copy))
        for head in range(HEADS_DEV):
            came = far_ref[move, head] if move < 2 else near_ref[0, head]
            rows_ref[move, head] = came * fade_ref[STEPS - 1:, head_slice(head)] + added_ref[move, head]

        @pl.when(valid)
        def _(copy=copy):
            copy.start()

    for valid, copy in copies:
        @pl.when(valid)
        def _(copy=copy):
            copy.wait()


def final_kernel(gate_ref, out_ref, square_a_ref, square_b_ref, new_ref, attended_ref):
    del new_ref
    scales = lax.rsqrt((square_a_ref[...] + square_b_ref[...]) * (1.0 / (HEADS * DK)) + epsilon)
    for slot in range(SLOTS_DEV):
        attended_ref[slot] = (out_ref[slot] * gate_ref[slot] * scales[:, slot:slot + 1]).astype(jnp.bfloat16)


def call(kernel, outs, in_specs, args, cost=100_000, limit=8, **more):
    return pl.pallas_call(
        kernel, out_shape=outs, in_specs=in_specs,
        compiler_params=pltpu.CompilerParams(vmem_limit_bytes=limit * 1024 * 1024),
        cost_estimate=pl.CostEstimate(flops=cost, bytes_accessed=cost, transcendentals=0), **more,
    )(*args)


def vmem(*shape, dtype=jnp.float32):
    return pltpu.VMEM(shape, dtype)


def in_hbm(*arrays):
    return tuple(pltpu.with_memory_space_constraint(x, pltpu.HBM) for x in arrays)


def over_rep(x, distance):
    return lax.ppermute(x, "rep", [(i, (i + distance) % N_REP) for i in range(N_REP)])


def over_head(x, flip):
    return lax.ppermute(x, "head", [(i, i ^ flip) for i in range(N_HEAD)])


def local(states, alive_flag, plan_source, plan_target, move_count, query_proj, key_proj, value_proj, gate_proj, decay_rate, norm_gain):
    row = (HEADS_DEV, DK, DK)
    features = (SLOTS_DEV, STEPS, WIDTH)
    source, target = plan_source.T, plan_target.T
    asked, info = call(
        ask_kernel, (vmem(2, STEPS, WIDTH), pltpu.SMEM((INFO,), jnp.int32)), [SMEM] * 3 + [VMEM],
        in_hbm(source, target, move_count, query_proj), out_specs=(VMEM, SMEM), cost=LONG)
    asked = over_rep(asked, FAR)
    far, near = call(
        outbox_kernel, (vmem(2, *row), vmem(1, *row)), [SMEM, ANY], (info, states), out_specs=(VMEM, VMEM),
        scratch_shapes=[pltpu.SemaphoreType.DMA((MOVE,))], cost=LONG)
    near = over_rep(near, 1)
    rows, near_query, fade, back = call(
        prepare_kernel, (pltpu.SMEM((ROWS,), jnp.int32), vmem(STEPS, WIDTH), vmem(STEPS, WIDTH), vmem(STEPS, WIDTH)),
        [SMEM] * 4 + [VMEM], (*in_hbm(alive_flag, move_count, decay_rate), info, query_proj), out_specs=(SMEM,) + (VMEM,) * 3)
    answer = call(answer_kernel, vmem(2, STEPS, WIDTH), [VMEM, VMEM, ANY], (asked, far, fade), out_specs=VMEM)
    part, arrives, gate, far = call(
        part_kernel, (vmem(*features), vmem(MOVE, SLOTS_DEV, STEPS, DK), vmem(*features), vmem(2, *row)),
        [SMEM] * 2 + [VMEM] * 7 + [ANY] * 2,
        (info, rows, fade, query_proj, key_proj, value_proj, gate_proj, norm_gain.reshape(1, WIDTH), states, answer, far),
        out_specs=(VMEM,) * 4, input_output_aliases={10: 3}, cost=LONG)
    answer = over_rep(answer, FAR)
    far = over_rep(far, FAR)
    out, square = call(
        combine_kernel, (vmem(*features), vmem(STEPS, DK)), [VMEM] * 6,
        (answer, near, near_query, part, arrives, fade), out_specs=(VMEM, VMEM), cost=LONG)
    new_states, added = call(
        state_kernel, (pltpu.HBM((SLOTS_DEV, *row), jnp.float32), vmem(MOVE, *row)), [SMEM] * 2 + [VMEM] * 5 + [ANY],
        (info, rows, fade, back, key_proj, value_proj, states, square), out_specs=(HBM, VMEM),
        scratch_shapes=[pltpu.VMEM((SLOTS_DEV, *row), jnp.float32), pltpu.SemaphoreType.DMA((SLOTS_DEV,))], cost=1_000_000)
    square = square + over_head(square, 1)
    square = call(add_kernel, vmem(STEPS, DK), [VMEM, VMEM, ANY], (square, over_head(square, 2), added), out_specs=VMEM)
    other = over_head(square, 6)
    new_states = call(
        update_kernel, jax.ShapeDtypeStruct((SLOTS_DEV, *row), jnp.float32), [SMEM] + [VMEM] * 4 + [ANY],
        (info, fade, added, far, near, new_states), out_specs=ANY, input_output_aliases={5: 0},
        scratch_shapes=[pltpu.VMEM((MOVE, *row), jnp.float32), pltpu.SemaphoreType.DMA((MOVE,))], cost=100_000)
    attended = call(
        final_kernel, jax.ShapeDtypeStruct(features, jnp.bfloat16), [VMEM] * 4 + [HBM], (gate, out, square, other, *in_hbm(new_states)),
        out_specs=VMEM)
    return attended, new_states


def solution(mesh):
    return jax.shard_map(
        local,
        mesh=mesh,
        in_specs=(
            P("rep", "head", None, None),
            P("rep"),
            P(),
            P(),
            P(),
            P("rep", None, "head"),
            P("rep", None, "head"),
            P("rep", None, "head"),
            P("rep", None, "head"),
            P("head"),
            P("head"),
        ),
        out_specs=(P("rep", None, "head"), P("rep", "head", None, None)),
        check_vma=False,
    )
```

```python
import jax
import jax.numpy as jnp
from jax import lax
from jax.experimental import pallas as pl
from jax.experimental.pallas import tpu as pltpu
from jax.sharding import PartitionSpec as P

SLOTS_DEV = 8
MOVE = 3
STEPS = 4
N_REP = 32
N_HEAD = 8
HEADS = 32
DK = 128
HEADS_DEV = HEADS // N_HEAD
WIDTH = HEADS_DEV * DK
FAR = N_REP // 2
epsilon = 1e-06

HIGHEST = lax.Precision.HIGHEST
VMEM = pl.BlockSpec(memory_space=pltpu.VMEM)
SMEM = pl.BlockSpec(memory_space=pltpu.SMEM)
ANY = pl.BlockSpec(memory_space=pl.ANY)
HBM = pl.BlockSpec(memory_space=pltpu.HBM)
LONG = 10_000_000_000


def silu(x):
    x = x.astype(jnp.float32)
    return x / (1.0 + jnp.exp(-x))


def sender_of(move):
    me = lax.axis_index("rep")
    return lax.rem(me + (FAR if move < 2 else N_REP - 1), N_REP)


SOURCE, VALID, SLOT, INFO = 0, MOVE, 2 * MOVE, 3 * MOVE
STAYS, LIVE, ROWS = 0, SLOTS_DEV, 2 * SLOTS_DEV


def split(x):
    high = x.astype(jnp.bfloat16)
    return high, (x - high.astype(jnp.float32)).astype(jnp.bfloat16)


def dot(a, b, dims):
    return lax.dot_general(a, b, (dims, ((), ())), preferred_element_type=jnp.float32)


def read_out(query, state):
    query_high, query_low = split(query)
    rows = jnp.concatenate([
        jnp.concatenate([query_high, query_high], axis=1), jnp.concatenate([query_low, jnp.zeros_like(query_low)], axis=1)], axis=0)
    both = dot(rows, jnp.concatenate(split(state), axis=0), ((1,), (0,)))
    return both[:STEPS] + both[STEPS:]


def later_by(x, gap):
    return x if gap == 0 else jnp.concatenate([jnp.zeros((gap, x.shape[1]), x.dtype), x[:-gap]], axis=0)


def head_slice(head):
    return slice(head * DK, (head + 1) * DK)


def times():
    return lax.broadcasted_iota(jnp.int32, (STEPS, DK), 0).astype(jnp.float32)


def ask_kernel(source_ref, target_ref, count_ref, query_ref, out_ref, info_ref):
    me = lax.axis_index("rep")
    for move in range(MOVE):
        sender = sender_of(move)
        slot = lax.rem(target_ref[move, sender], SLOTS_DEV)
        if move < 2:
            out_ref[move] = silu(query_ref[slot])
        info_ref[SOURCE + move] = source_ref[move, me]
        info_ref[VALID + move] = (count_ref[sender] > move).astype(jnp.int32)
        info_ref[SLOT + move] = slot


def prepare_kernel(alive_ref, count_ref, rate_ref, info_ref, query_ref, rows_ref, near_query_ref, fade_ref, back_ref):
    count = count_ref[lax.axis_index("rep")]
    near_query_ref[...] = silu(query_ref[info_ref[SLOT + 2]])
    for slot in range(SLOTS_DEV):
        stays = alive_ref[slot]
        for move in range(MOVE):
            stays = jnp.where((count > move) & (info_ref[SOURCE + move] == slot), 0, stays)
        live = stays
        for move in range(MOVE):
            live = jnp.where((info_ref[VALID + move] == 1) & (info_ref[SLOT + move] == slot), 1, live)
        rows_ref[STAYS + slot] = stays
        rows_ref[LIVE + slot] = live
    for head in range(HEADS_DEV):
        fade_ref[:, head_slice(head)] = jnp.exp(-rate_ref[head] * (times() + 1.0))
        back_ref[:, head_slice(head)] = jnp.exp(-rate_ref[head] * (STEPS - 1.0 - times()))


def outbox_kernel(info_ref, states_ref, far_ref, near_ref, sems):
    copies = []
    for move in range(MOVE):
        out = far_ref.at[move] if move < 2 else near_ref.at[0]
        copies.append(pltpu.make_async_copy(states_ref.at[info_ref[SOURCE + move]], out, sems.at[move]))
    for copy in copies:
        copy.start()
    for copy in copies:
        copy.wait()


def answer_kernel(query_ref, far_ref, fade_ref, out_ref):
    del fade_ref
    for move in range(2):
        for head in range(HEADS_DEV):
            out_ref[move, :, head_slice(head)] = read_out(query_ref[move, :, head_slice(head)], far_ref[move, head])


def part_kernel(
    info_ref, flags_ref, fade_ref, query_ref, key_ref, value_ref, gate_ref, gain_ref, states_ref, answer_ref, far_in_ref,
    out_ref, flag_ref, gate_out_ref, far_ref,
):
    del answer_ref, far_in_ref, far_ref
    for slot in range(SLOTS_DEV):
        for move in range(MOVE):
            arrives = info_ref[VALID + move] * (info_ref[SLOT + move] == slot).astype(jnp.int32)
            flag_ref[move, slot] = jnp.full((STEPS, DK), arrives.astype(jnp.float32))
        live = flags_ref[LIVE + slot].astype(jnp.float32)
        stays = flags_ref[STAYS + slot].astype(jnp.float32)
        gate_out_ref[slot] = gain_ref[...] * live / (1.0 + jnp.exp(-gate_ref[slot].astype(jnp.float32)))
        queries, keys, values = silu(query_ref[slot]), silu(key_ref[slot]), silu(value_ref[slot])
        inside = [jnp.zeros((STEPS, DK), jnp.float32)] * HEADS_DEV
        for gap in range(STEPS):
            older_keys, older_values = later_by(keys, gap), later_by(values, gap)
            if gap:
                older_values = older_values * fade_ref[gap - 1:gap]
            for head in range(HEADS_DEV):
                at = head_slice(head)
                inside[head] += jnp.sum(queries[:, at] * older_keys[:, at], axis=1, keepdims=True) * older_values[:, at]
        for head in range(HEADS_DEV):
            at = head_slice(head)
            before = read_out(queries[:, at], states_ref[slot, head])
            out_ref[slot, :, at] = inside[head] + before * (fade_ref[:, at] * stays)


def state_kernel(
    info_ref, flags_ref, fade_ref, back_ref, key_ref, value_ref, states_ref, square_ref,
    new_ref, added_ref, rows_ref, sems,
):
    del square_ref
    copies = []
    for slot in range(SLOTS_DEV):
        live = flags_ref[LIVE + slot].astype(jnp.float32)
        stays = flags_ref[STAYS + slot].astype(jnp.float32)
        keys, values = silu(key_ref[slot]) * (back_ref[...] * live), silu(value_ref[slot])
        for head in range(HEADS_DEV):
            at = head_slice(head)
            value_high, value_low = split(values[:, at])
            faded_high, faded_low = split(keys[:, at])
            added = dot(
                jnp.concatenate([faded_high, faded_low, faded_high], axis=0),
                jnp.concatenate([value_high, value_high, value_low], axis=0), ((0,), (0,)))
            rows_ref[slot, head] = states_ref[slot, head] * (fade_ref[STEPS - 1:, at] * stays) + added
        copies.append(pltpu.make_async_copy(rows_ref.at[slot], new_ref.at[slot], sems.at[slot]))
        copies[-1].start()
    for move in range(MOVE):
        @pl.when(info_ref[VALID + move] == 1)
        def _(move=move):
            added_ref[move] = rows_ref[info_ref[SLOT + move]]

    for copy in copies:
        copy.wait()


def combine_kernel(answer_ref, near_ref, near_query_ref, part_ref, flag_ref, fade_ref, out_ref, square_ref):
    moved = [answer_ref[0], answer_ref[1], jnp.concatenate(
        [read_out(near_query_ref[:, head_slice(head)], near_ref[0, head]) for head in range(HEADS_DEV)], axis=1)]
    moved = [x * fade_ref[...] for x in moved]
    lanes = lax.broadcasted_iota(jnp.int32, (STEPS, DK), 1)
    squares = jnp.zeros((STEPS, DK), jnp.float32)
    for slot in range(SLOTS_DEV):
        total = jnp.zeros((STEPS, DK), jnp.float32)
        for head in range(HEADS_DEV):
            at = head_slice(head)
            row = part_ref[slot, :, at]
            for move in range(MOVE):
                row += flag_ref[move, slot] * moved[move][:, at]
            out_ref[slot, :, at] = row
            total += row * row
        squares = jnp.where(lanes == slot, jnp.sum(total, axis=1, keepdims=True), squares)
    square_ref[...] = squares


def add_kernel(a_ref, b_ref, added_ref, out_ref):
    del added_ref
    out_ref[...] = a_ref[...] + b_ref[...]


def update_kernel(info_ref, fade_ref, added_ref, far_ref, near_ref, old_ref, new_ref, rows_ref, sems):
    del old_ref
    copies = []
    for move in range(MOVE):
        valid = info_ref[VALID + move] == 1
        copy = pltpu.make_async_copy(rows_ref.at[move], new_ref.at[info_ref[SLOT + move]], sems.at[move])
        copies.append((valid, copy))
        for head in range(HEADS_DEV):
            came = far_ref[move, head] if move < 2 else near_ref[0, head]
            rows_ref[move, head] = came * fade_ref[STEPS - 1:, head_slice(head)] + added_ref[move, head]

        @pl.when(valid)
        def _(copy=copy):
            copy.start()

    for valid, copy in copies:
        @pl.when(valid)
        def _(copy=copy):
            copy.wait()


def final_kernel(gate_ref, out_ref, square_a_ref, square_b_ref, new_ref, attended_ref):
    del new_ref
    scales = lax.rsqrt((square_a_ref[...] + square_b_ref[...]) * (1.0 / (HEADS * DK)) + epsilon)
    for slot in range(SLOTS_DEV):
        attended_ref[slot] = (out_ref[slot] * gate_ref[slot] * scales[:, slot:slot + 1]).astype(jnp.bfloat16)


def call(kernel, outs, in_specs, args, cost=100_000, limit=8, **more):
    return pl.pallas_call(
        kernel, out_shape=outs, in_specs=in_specs,
        compiler_params=pltpu.CompilerParams(vmem_limit_bytes=limit * 1024 * 1024),
        cost_estimate=pl.CostEstimate(flops=cost, bytes_accessed=cost, transcendentals=0), **more,
    )(*args)


def vmem(*shape, dtype=jnp.float32):
    return pltpu.VMEM(shape, dtype)


def in_hbm(*arrays):
    return tuple(pltpu.with_memory_space_constraint(x, pltpu.HBM) for x in arrays)


def over_rep(x, distance):
    return lax.ppermute(x, "rep", [(i, (i + distance) % N_REP) for i in range(N_REP)])


def over_head(x, flip):
    return lax.ppermute(x, "head", [(i, i ^ flip) for i in range(N_HEAD)])


def local(states, alive_flag, plan_source, plan_target, move_count, query_proj, key_proj, value_proj, gate_proj, decay_rate, norm_gain):
    row = (HEADS_DEV, DK, DK)
    features = (SLOTS_DEV, STEPS, WIDTH)
    source, target = plan_source.T, plan_target.T
    asked, info = call(
        ask_kernel, (vmem(2, STEPS, WIDTH), pltpu.SMEM((INFO,), jnp.int32)), [SMEM] * 3 + [VMEM],
        in_hbm(source, target, move_count, query_proj), out_specs=(VMEM, SMEM), cost=LONG)
    asked = over_rep(asked, FAR)
    far, near = call(
        outbox_kernel, (vmem(2, *row), vmem(1, *row)), [SMEM, ANY], (info, states), out_specs=(VMEM, VMEM),
        scratch_shapes=[pltpu.SemaphoreType.DMA((MOVE,))], cost=LONG)
    near = over_rep(near, 1)
    rows, near_query, fade, back = call(
        prepare_kernel, (pltpu.SMEM((ROWS,), jnp.int32), vmem(STEPS, WIDTH), vmem(STEPS, WIDTH), vmem(STEPS, WIDTH)),
        [SMEM] * 4 + [VMEM], (*in_hbm(alive_flag, move_count, decay_rate), info, query_proj), out_specs=(SMEM,) + (VMEM,) * 3)
    answer = call(answer_kernel, vmem(2, STEPS, WIDTH), [VMEM, VMEM, ANY], (asked, far, fade), out_specs=VMEM)
    part, arrives, gate, far = call(
        part_kernel, (vmem(*features), vmem(MOVE, SLOTS_DEV, STEPS, DK), vmem(*features), vmem(2, *row)),
        [SMEM] * 2 + [VMEM] * 7 + [ANY] * 2,
        (info, rows, fade, query_proj, key_proj, value_proj, gate_proj, norm_gain.reshape(1, WIDTH), states, answer, far),
        out_specs=(VMEM,) * 4, input_output_aliases={10: 3}, cost=LONG)
    answer = over_rep(answer, FAR)
    far = over_rep(far, FAR)
    out, square = call(
        combine_kernel, (vmem(*features), vmem(STEPS, DK)), [VMEM] * 6,
        (answer, near, near_query, part, arrives, fade), out_specs=(VMEM, VMEM), cost=LONG)
    new_states, added = call(
        state_kernel, (pltpu.HBM((SLOTS_DEV, *row), jnp.float32), vmem(MOVE, *row)), [SMEM] * 2 + [VMEM] * 5 + [ANY],
        (info, rows, fade, back, key_proj, value_proj, states, square), out_specs=(HBM, VMEM),
        scratch_shapes=[pltpu.VMEM((SLOTS_DEV, *row), jnp.float32), pltpu.SemaphoreType.DMA((SLOTS_DEV,))], cost=1_000_000)
    square = square + over_head(square, 1)
    square = call(add_kernel, vmem(STEPS, DK), [VMEM, VMEM, ANY], (square, over_head(square, 2), added), out_specs=VMEM)
    other = over_head(square, 6)
    new_states = call(
        update_kernel, jax.ShapeDtypeStruct((SLOTS_DEV, *row), jnp.float32), [SMEM] + [VMEM] * 4 + [ANY],
        (info, fade, added, far, near, new_states), out_specs=ANY, input_output_aliases={5: 0},
        scratch_shapes=[pltpu.VMEM((MOVE, *row), jnp.float32), pltpu.SemaphoreType.DMA((MOVE,))], cost=100_000)
    attended = call(
        final_kernel, jax.ShapeDtypeStruct(features, jnp.bfloat16), [VMEM] * 4 + [HBM], (gate, out, square, other, *in_hbm(new_states)),
        out_specs=VMEM)
    return attended, new_states


def solution(mesh):
    return jax.shard_map(
        local,
        mesh=mesh,
        in_specs=(
            P("rep", "head", None, None),
            P("rep"),
            P(),
            P(),
            P(),
            P("rep", None, "head"),
            P("rep", None, "head"),
            P("rep", None, "head"),
            P("rep", None, "head"),
            P("head"),
            P("head"),
        ),
        out_specs=(P("rep", None, "head"), P("rep", "head", None, None)),
        check_vma=False,
    )
```
